512 devices in a mesh: tm: 32 (over x, y, core), space: 16 (over z).
Axes of the slice: x: 4, y: 4, z: 16, core: 2. Of those that a mesh axis runs over, the one named last changes fastest.
Arguments:
- video_tokens: bfloat16 [32, 64, 64, 1152], P('tm', 'space'), may hold values from -6 to 6
- qkv_weight: bfloat16 [1152, 3456], P('space'), may hold values from -0.1875 to 0.1875
- out_weight: bfloat16 [1152, 1152], P('space'), may hold values from -0.1875 to 0.1875
- conv_weight: float32 [3, 3, 1152], replicated, may hold values from -2 to 2
- norm_gain: float32 [1152], replicated, may hold values from 0.1 to 1.9
Outputs:
- attended: bfloat16 [32, 64, 64, 1152], P('tm', 'space')
The draws below stay inside these ranges and needn't reach their ends.
All inputs are finite; a program needn't handle non-finite values.
Results may differ from the reference program's by a relative error of at most 0.015.
Values may be sent and summed in bfloat16 or wider, within the bound.
A program may use at most 64 MiB of HBM per device.

```python
import jax
import jax.numpy as jnp
from jax import lax

HEADS = 36
HEAD_DIM = 32
D = 1152
COLS = 64
ROWS = 64
FRAMES = 32


def levels(key, shape, split, least, top_value):
    factor_of = 1.0
    for axis_at, parts in split:
        steps = jax.random.uniform(jax.random.fold_in(jax.random.fold_in(key, 6), axis_at), (parts,), jnp.float32, least / len(split), top_value / len(split))
        factor_of = factor_of * jnp.repeat(jnp.exp(steps), shape[axis_at] // parts).reshape((-1,) + (1,) * (len(shape) - 1 - axis_at))
    return factor_of


def noise(rng, extent, spread, reach, cuts=(), dtype=jnp.bfloat16):
    values = spread * jax.random.normal(rng, extent, jnp.float32)
    if cuts:
        values = values * levels(rng, extent, cuts, -0.22, 0.18)
    return jnp.clip(values, -reach, reach).astype(dtype)


def setup_inputs(seed: int = 0) -> dict:
    streams_of = jax.random.split(jax.random.key(seed), 6)
    return {
        "video_tokens": noise(streams_of[0], (FRAMES, ROWS, COLS, D), 1.0, 6.0, ((0, 32), (1, 16))),
        "qkv_weight": noise(streams_of[1], (D, 3 * D), D ** -0.5, 0.1875, ((0, 16),)),
        "out_weight": noise(streams_of[2], (D, D), D ** -0.5, 0.1875, ((0, 16),)),
        "conv_weight": noise(streams_of[3], (3, 3, D), 9 ** -0.5, 2.0, (), jnp.float32),
        "norm_gain": jnp.clip(1.0 + 0.18 * jax.random.normal(streams_of[4], (D,), jnp.float32), 0.1, 1.9),
    }


def project_frame(frame_tokens, qkv_weight):
    feat_width = frame_tokens.shape[-1]
    flat_tokens = frame_tokens.reshape(-1, feat_width)
    projected = jnp.dot(flat_tokens, qkv_weight, preferred_element_type=jnp.float32)
    query_feat = lax.optimization_barrier(jax.nn.relu(projected[:, :feat_width]).astype(jnp.bfloat16))
    key_feat = lax.optimization_barrier(jax.nn.relu(projected[:, feat_width:2 * feat_width]).astype(jnp.bfloat16))
    values = lax.optimization_barrier(projected[:, 2 * feat_width:].astype(jnp.bfloat16))
    key_heads = key_feat.astype(jnp.float32).reshape(-1, HEADS, HEAD_DIM)
    value_heads = values.astype(jnp.float32).reshape(-1, HEADS, HEAD_DIM)
    frame_state = jnp.einsum('thd,the->hde', key_heads, value_heads, precision=lax.Precision.HIGHEST)
    return (query_feat, values, frame_state)

def finish_frame(query_feat, values, causal_state, out_weight, conv_weight, norm_gain):
    feat_width = query_feat.shape[-1]
    state_low = lax.optimization_barrier(causal_state.astype(jnp.bfloat16))
    query_heads = query_feat.astype(jnp.float32).reshape(-1, HEADS, HEAD_DIM)
    readout = jnp.einsum('thd,hde->the', query_heads, state_low.astype(jnp.float32), precision=lax.Precision.HIGHEST)
    readout = readout.reshape(-1, feat_width)
    mean_square = lax.optimization_barrier(jnp.mean(readout * readout, axis=-1, keepdims=True))
    normed = readout * lax.rsqrt(mean_square + 1e-06) * norm_gain
    value_grid = values.astype(jnp.float32).reshape(ROWS, COLS, feat_width)
    padded = jnp.pad(value_grid, ((1, 1), (1, 1), (0, 0)))
    local_term = jnp.zeros((ROWS, COLS, feat_width), jnp.float32)
    for row_shift in range(3):
        for col_shift in range(3):
            local_term = local_term + conv_weight[row_shift, col_shift] * padded[row_shift:row_shift + ROWS, col_shift:col_shift + COLS]
    mixture = (normed + local_term.reshape(-1, feat_width)).astype(jnp.bfloat16)
    result = jnp.dot(mixture, out_weight, preferred_element_type=jnp.float32).astype(jnp.bfloat16)
    return result.reshape(ROWS, COLS, feat_width)

def reference(video_tokens, qkv_weight, out_weight, conv_weight, norm_gain):
    query_all, value_all, frame_states = lax.map(lambda frame_tokens: project_frame(frame_tokens, qkv_weight), video_tokens)
    causal_states = jnp.cumsum(frame_states, axis=0)

    def finish_one(packed):
        return finish_frame(packed[0], packed[1], packed[2], out_weight, conv_weight, norm_gain)
    return lax.map(finish_one, (query_all, value_all, causal_states))
```

```python
import jax
import jax.numpy as jnp
from jax import lax
from jax.experimental import pallas as pl
from jax.experimental.pallas import tpu as pltpu
from jax.sharding import PartitionSpec as P

MESH = pl.DeviceIdType.MESH
D = 1152
ROWS = 72
TOKENS = 256
COLS = 64
NZ = 16
TILES = 9
LANES = 128
LAG = 2
LOWEST = -3.0e38
EPS = 1e-06


def kernel(
    tok_ref, qkv_ref, ow_ref, conv_ref, gain_ref, out_ref,
    wkv, wqo, wo, wo_flat, tsib, split, acc, kvb, qb, stage, halo, local,
    part_low, a_in, f_in, b_in, chip_low, c_in, readout, mix,
    zkv_s, zkv_r, zqo_s, zqo_r, kvs_s, kvs_r, qos_s, qos_r,
    tok_sem, kv_sem, q_sem, o_sem, halo_s, halo_r, a_s, a_r, f_sem, b_s, b_r, c_s, c_r,
):
    tm = lax.axis_index("tm")
    z = lax.axis_index("space")
    core = lax.rem(tm, 2)
    chip = tm // 2
    x = chip // 4
    y = lax.rem(chip, 4)

    def at(px, py, pc, pz):
        return ((px * 4 + py) * 2 + pc, pz)

    def x_off(i):
        return at(lax.rem(x + i + 4, 4), y, core, z)

    def y_off(i):
        return at(x, lax.rem(y + i + 4, 4), core, z)

    def z_off(i):
        return at(x, y, core, lax.rem(z + i + NZ, NZ))

    sibling = at(x, y, 1 - core, z)

    def remote(src, dst, ssem, rsem, device):
        return pltpu.make_async_remote_copy(
            src_ref=src, dst_ref=dst, send_sem=ssem, recv_sem=rsem,
            device_id=device, device_id_type=MESH,
        )

    slot_tile = [0, 1 + x, 5 + y]
    slot_tile += [1 + lax.rem(x + i, 4) for i in (1, 2, 3)]
    slot_tile += [5 + lax.rem(y + i, 4) for i in (1, 2, 3)]

    def lanes(slot):
        return pl.ds(slot * LANES, LANES)

    def tile_lanes(tile):
        return pl.ds(pl.multiple_of(tile * LANES, LANES), LANES)

    peers = [z_off(1), z_off(-1), sibling]
    peers += [x_off(i) for i in (1, 2, 3)] + [y_off(i) for i in (1, 2, 3)]
    barrier = pltpu.get_barrier_semaphore()
    for peer in peers:
        pl.semaphore_signal(barrier, inc=1, device_id=peer, device_id_type=MESH)

    for slot in range(TILES):
        tile = slot_tile[slot]
        offset = (1 + core) * TILES + tile
        wkv[z, :, lanes(slot)] = qkv_ref[:, tile_lanes(offset)]

    @pl.when(core == 0)
    def _():
        for slot in range(TILES):
            wqo[z, :, lanes(slot)] = qkv_ref[:, tile_lanes(slot_tile[slot])]

    @pl.when(core == 1)
    def _():
        for slot in range(TILES):
            wqo[z, :, lanes(slot)] = ow_ref[:, tile_lanes(slot_tile[slot])]

    pl.semaphore_wait(barrier, len(peers))

    def z_kv(way, s, t, source):
        ref = wkv.at[source, :, lanes(t)]
        return remote(ref, ref, zkv_s.at[way, s - 1, t], zkv_r.at[way, s - 1, t], z_off(1 - 2 * way))

    def z_qo(way, s, source):
        ref = wqo.at[source, :, pl.ds(0, 3 * LANES)]
        return remote(ref, ref, zqo_s.at[way, s - 1], zqo_r.at[way, s - 1], z_off(1 - 2 * way))

    def share(buf, ssem, rsem, way, s, source, line, i):
        device = x_off(-i) if line == 0 else y_off(-i)
        at_sem = (way, s - 1, 3 * line + i - 1)
        return remote(
            buf.at[source, :, lanes(1 + line)], buf.at[source, :, lanes(2 + 3 * line + i)],
            ssem.at[at_sem], rsem.at[at_sem], device,
        )

    def source_of(way, s):
        return lax.rem(z + NZ - s, NZ) if way == 0 else lax.rem(z + s, NZ)

    for t in range(3):
        for way in range(2):
            z_kv(way, 1, t, z).start()
    token_swap = remote(tok_ref, tsib, tok_sem.at[0], tok_sem.at[1], sibling)
    token_swap.start()
    for way in range(2):
        z_qo(way, 1, z).start()

    for block in range(NZ):
        split[block, 0:TOKENS, :] = tok_ref[:, block * ROWS : (block + 1) * ROWS]
    token_swap.wait()
    for block in range(NZ):
        split[block, TOKENS : 2 * TOKENS, :] = tsib[:, block * ROWS : (block + 1) * ROWS]

    def add_source(buf, source, first):
        left = split[source]
        for n in range(3):
            cols = pl.ds(n * 3 * LANES, 3 * LANES)
            term = jnp.dot(left, buf[source, :, cols], preferred_element_type=jnp.float32)
            acc[:, cols] = term if first else acc[:, cols] + term

    add_source(wkv, z, True)

    def ring(s, carry):
        for way in range(2):
            @pl.when(s <= 8 - way)
            def _():
                source = source_of(way, s)
                for t in (1, 2, 0):
                    z_kv(way, s, t, source).wait_recv()

                    @pl.when(s < 8 - way)
                    def _():
                        z_kv(way, s + 1, t, source).start()

                    if t > 0:
                        for i in (1, 2, 3):
                            share(wkv, kvs_s, kvs_r, way, s, source, t - 1, i).start()

        late = s - LAG
        for way in range(2):
            @pl.when((late >= 1) & (late <= 8 - way))
            def _():
                source = source_of(way, late)
                z_qo(way, late, source).wait_recv()

                @pl.when(late < 8 - way)
                def _():
                    z_qo(way, late + 1, source).start()

                for line in range(2):
                    for i in (1, 2, 3):
                        share(wqo, qos_s, qos_r, way, late, source, line, i).start()

                for line in range(2):
                    for i in (1, 2, 3):
                        share(wkv, kvs_s, kvs_r, way, late, source, line, i).wait_recv()
                add_source(wkv, source, False)

        return carry

    lax.fori_loop(1, 9 + LAG, ring, 0)

    floor = jnp.where(core == 0, 0.0, LOWEST).astype(jnp.float32)
    swaps = []
    for n in range(3):
        for k in range(3):
            slot = 3 * n + k
            stage[n, :, lanes(k)] = jnp.maximum(acc[TOKENS:, lanes(slot)], floor).astype(jnp.bfloat16)
        swap = remote(stage.at[n], stage.at[3 + n], kv_sem.at[n], kv_sem.at[3 + n], sibling)
        swap.start()
        swaps.append(swap)
    for slot in range(TILES):
        kvb[core, :, tile_lanes(slot_tile[slot])] = jnp.maximum(
            acc[0:TOKENS, lanes(slot)], floor
        ).astype(jnp.bfloat16)
    for n in range(3):
        swaps[n].wait()
        for k in range(3):
            slot = 3 * n + k
            kvb[1 - core, :, tile_lanes(slot_tile[slot])] = stage[3 + n, :, lanes(k)]

    down = remote(kvb.at[1, pl.ds(3 * COLS, COLS)], halo.at[0], halo_s.at[0], halo_r.at[0], z_off(1))
    up = remote(kvb.at[1, pl.ds(0, COLS)], halo.at[1], halo_s.at[1], halo_r.at[1], z_off(-1))

    row_head = lax.broadcasted_iota(jnp.int32, (LANES, LANES), 0) // 32
    col_head = lax.broadcasted_iota(jnp.int32, (LANES, LANES), 1) // 32
    same_head = row_head == col_head

    def a_copy(j):
        return remote(part_low.at[j], a_in.at[z], a_s.at[j], a_r.at[z], at(x, y, core, j))

    for j in range(TILES):
        gram = lax.dot_general(
            kvb[0, :, lanes(j)], kvb[1, :, lanes(j)], (((0,), (0,)), ((), ())),
            preferred_element_type=jnp.float32,
        )
        gram = jnp.where(same_head, gram, 0.0)
        part = gram[0:32] + gram[32:64] + gram[64:96] + gram[96:128]
        part_low[j] = part.astype(jnp.bfloat16)

        @pl.when(z != j)
        def _():
            a_copy(j).start()

    @pl.when(z < NZ - 1)
    def _():
        down.start()

    @pl.when(z > 0)
    def _():
        up.start()

    def wait_shares(s, carry):
        for way in range(2):
            @pl.when(s <= 8 - way)
            def _():
                source = source_of(way, s)
                for line in range(2):
                    for i in (1, 2, 3):
                        share(wqo, qos_s, qos_r, way, s, source, line, i).wait_recv()
        return carry

    lax.fori_loop(1, 9, wait_shares, 0)

    o_send = remote(wqo, wo, o_sem.at[0], o_sem.at[1], sibling)
    q_send = remote(qb.at[1], qb.at[0], q_sem.at[0], q_sem.at[1], sibling)

    @pl.when(core == 1)
    def _():
        o_send.start()

    @pl.when(core == 0)
    def _():
        add_source(wqo, 0, True)

        def more(source, carry):
            add_source(wqo, source, False)
            return carry

        lax.fori_loop(1, NZ, more, 0)
        for slot in range(TILES):
            qb[1, :, tile_lanes(slot_tile[slot])] = jnp.maximum(
                acc[TOKENS:, lanes(slot)], 0.0
            ).astype(jnp.bfloat16)
        q_send.start()
        for slot in range(TILES):
            qb[0, :, tile_lanes(slot_tile[slot])] = jnp.maximum(
                acc[0:TOKENS, lanes(slot)], 0.0
            ).astype(jnp.bfloat16)

    def f_copy():
        return remote(f_in.at[0], f_in.at[1], f_sem.at[0], f_sem.at[1], sibling)

    def b_copy(i):
        later = chip + i
        return remote(
            chip_low, b_in.at[i - 1], b_s.at[i - 1], b_r.at[i - 1], (later * 2 + core, z)
        )

    def c_copy(j):
        return remote(c_in.at[z], c_in.at[z], c_s.at[j], c_r.at[z], at(x, y, core, j))

    @pl.when(z < TILES)
    def _():
        f_in[0] = part_low[z].astype(jnp.float32)

        def gather(k, carry):
            source = lax.rem(z + k, NZ)
            remote(part_low.at[0], a_in.at[source], a_s.at[0], a_r.at[source], z_off(1)).wait_recv()
            f_in[0] = f_in[0] + a_in[source].astype(jnp.float32)
            return carry

        lax.fori_loop(1, NZ, gather, 0)
        swap = f_copy()
        swap.start()
        swap.wait()
        chip_low[...] = (f_in[0] + f_in[1]).astype(jnp.bfloat16)
        for i in range(1, NZ):
            @pl.when(chip + i < NZ)
            def _():
                b_copy(i).start()
        readout[0:32, 0:LANES] = f_in[0] + jnp.where(core == 1, f_in[1], 0.0)
        for i in range(1, NZ):
            @pl.when(chip >= i)
            def _():
                b_copy(i).wait_recv()
                readout[0:32, 0:LANES] += b_in[i - 1].astype(jnp.float32)
        c_in[z] = readout[0:32, 0:LANES].astype(jnp.bfloat16)
        for j in range(NZ):
            @pl.when(z != j)
            def _():
                c_copy(j).start()

    @pl.when(z > 0)
    def _():
        down.wait_recv()

    @pl.when(z == 0)
    def _():
        halo[0] = jnp.zeros((COLS, D), jnp.bfloat16)

    @pl.when(z < NZ - 1)
    def _():
        up.wait_recv()

    @pl.when(z == NZ - 1)
    def _():
        halo[1] = jnp.zeros((COLS, D), jnp.bfloat16)

    col = lax.broadcasted_iota(jnp.int32, (COLS, LANES), 0)

    def conv(j, carry):
        cols = tile_lanes(j)
        weight = conv_ref[:, cols]
        sums = [jnp.zeros((COLS, LANES), jnp.float32) for _ in range(4)]
        for row in range(6):
            if row == 0:
                mid = halo[0, :, cols]
            elif row == 5:
                mid = halo[1, :, cols]
            else:
                mid = kvb[1, pl.ds((row - 1) * COLS, COLS), cols]
            mid = mid.astype(jnp.float32)
            left = jnp.where(col == 0, 0.0, pltpu.roll(mid, 1, 0))
            right = jnp.where(col == COLS - 1, 0.0, pltpu.roll(mid, COLS - 1, 0))
            for a in range(3):
                r = row - a
                if 0 <= r < 4:
                    sums[r] = (
                        sums[r] + weight[3 * a] * left + weight[3 * a + 1] * mid
                        + weight[3 * a + 2] * right
                    )
        for r in range(4):
            local[pl.ds(r * COLS, COLS), cols] = sums[r]
        return carry

    lax.fori_loop(0, TILES, conv, 0)

    @pl.when(core == 0)
    def _():
        o_send.wait_recv()

    def flatten(buf):
        def pair(k, carry):
            for slot in range(TILES):
                both = jnp.concatenate(
                    [
                        buf[2 * k, :, lanes(slot)].astype(jnp.float32),
                        buf[2 * k + 1, :, lanes(slot)].astype(jnp.float32),
                    ],
                    axis=0,
                )
                rows = pl.ds(pl.multiple_of(k * 2 * ROWS, 16), 2 * ROWS)
                wo_flat[rows, lanes(slot)] = both.astype(jnp.bfloat16)
            return carry

        lax.fori_loop(0, NZ // 2, pair, 0)

    @pl.when(core == 0)
    def _():
        flatten(wo)

    @pl.when(core == 1)
    def _():
        flatten(wqo)
        q_send.wait_recv()

    for j in range(TILES):
        @pl.when(z != j)
        def _():
            remote(c_in.at[j], c_in.at[j], c_s.at[j], c_r.at[j], z_off(1)).wait_recv()

    square = jnp.zeros((TOKENS, LANES), jnp.float32)
    for j in range(TILES):
        state = jnp.concatenate([c_in[j].astype(jnp.float32)] * 4, axis=0)
        state = jnp.where(same_head, state, 0.0).astype(jnp.bfloat16)
        term = jnp.dot(qb[0, :, lanes(j)], state, preferred_element_type=jnp.float32)
        readout[:, lanes(j)] = term
        square = square + term * term
    mean_square = jnp.sum(square, axis=-1, keepdims=True) * (1.0 / D)
    scale = lax.rsqrt(mean_square + EPS)
    for j in range(TILES):
        normed = readout[:, lanes(j)] * scale * gain_ref[:, lanes(j)]
        mix[:, lanes(j)] = (normed + local[:, lanes(j)]).astype(jnp.bfloat16)
    for n in range(3):
        cols = pl.ds(n * 3 * LANES, 3 * LANES)
        result = jnp.dot(mix[...], wo_flat[:, cols], preferred_element_type=jnp.float32)
        result = result.astype(jnp.bfloat16)
        for k in range(3):
            out_ref[:, tile_lanes(slot_tile[3 * n + k])] = result[:, k * LANES : (k + 1) * LANES]

    def sends(s, carry):
        for way in range(2):
            @pl.when(s <= 8 - way)
            def _():
                source = source_of(way, s)
                for t in range(3):
                    z_kv(way, s, t, source).wait_send()
                z_qo(way, s, source).wait_send()
                for line in range(2):
                    for i in (1, 2, 3):
                        share(wkv, kvs_s, kvs_r, way, s, source, line, i).wait_send()
                        share(wqo, qos_s, qos_r, way, s, source, line, i).wait_send()
        return carry

    lax.fori_loop(1, 9, sends, 0)
    for j in range(TILES):
        @pl.when(z != j)
        def _():
            a_copy(j).wait_send()

    @pl.when(z < NZ - 1)
    def _():
        down.wait_send()

    @pl.when(z > 0)
    def _():
        up.wait_send()

    @pl.when(core == 1)
    def _():
        o_send.wait_send()

    @pl.when(core == 0)
    def _():
        q_send.wait_send()

    @pl.when(z < TILES)
    def _():
        for i in range(1, NZ):
            @pl.when(chip + i < NZ)
            def _():
                b_copy(i).wait_send()
        for j in range(NZ):
            @pl.when(z != j)
            def _():
                c_copy(j).wait_send()


def per_device(video_tokens, qkv_weight, out_weight, conv_weight, norm_gain):
    tokens = video_tokens.reshape(TOKENS, D)
    bf16, f32 = jnp.bfloat16, jnp.float32
    vmem = pl.BlockSpec(memory_space=pltpu.VMEM)
    dma = pltpu.SemaphoreType.DMA
    result = pl.pallas_call(
        kernel,
        out_shape=jax.ShapeDtypeStruct((TOKENS, D), bf16),
        in_specs=[vmem] * 5,
        out_specs=vmem,
        scratch_shapes=[
            pltpu.VMEM((NZ, ROWS, D), bf16),
            pltpu.VMEM((NZ, ROWS, D), bf16),
            pltpu.VMEM((NZ, ROWS, D), bf16),
            pltpu.VMEM((D, D), bf16),
            pltpu.VMEM((TOKENS, D), bf16),
            pltpu.VMEM((NZ, 2 * TOKENS, ROWS), bf16),
            pltpu.VMEM((2 * TOKENS, D), f32),
            pltpu.VMEM((2, TOKENS, D), bf16),
            pltpu.VMEM((2, TOKENS, D), bf16),
            pltpu.VMEM((6, TOKENS, 3 * LANES), bf16),
            pltpu.VMEM((2, COLS, D), bf16),
            pltpu.VMEM((TOKENS, D), f32),
            pltpu.VMEM((TILES, 32, LANES), bf16),
            pltpu.VMEM((NZ, 32, LANES), bf16),
            pltpu.VMEM((2, 32, LANES), f32),
            pltpu.VMEM((NZ - 1, 32, LANES), bf16),
            pltpu.VMEM((32, LANES), bf16),
            pltpu.VMEM((TILES, 32, LANES), bf16),
            pltpu.VMEM((TOKENS, D), f32),
            pltpu.VMEM((TOKENS, D), bf16),
            dma((2, 8, 3)), dma((2, 8, 3)),
            dma((2, 8)), dma((2, 8)),
            dma((2, 8, 6)), dma((2, 8, 6)),
            dma((2, 8, 6)), dma((2, 8, 6)),
            dma((2,)),
            dma((6,)),
            dma((2,)),
            dma((2,)),
            dma((2,)), dma((2,)),
            dma((TILES,)), dma((NZ,)),
            dma((2,)),
            dma((NZ - 1,)), dma((NZ - 1,)),
            dma((NZ,)), dma((TILES,)),
        ],
        compiler_params=pltpu.CompilerParams(
            collective_id=0, has_side_effects=True, vmem_limit_bytes=48 * 2**20
        ),
        name="block",
    )(tokens, qkv_weight, out_weight, conv_weight.reshape(9, D), norm_gain.reshape(1, D))
    return result.reshape(video_tokens.shape)


def solution(mesh):
    in_specs = (P("tm", "space", None, None), P("space", None), P("space", None), P(), P())
    out_specs = P("tm", "space", None, None)
    return jax.shard_map(
        per_device, mesh=mesh, in_specs=in_specs, out_specs=out_specs, check_vma=False
    )
```

```python
import jax
import jax.numpy as jnp
from jax import lax
from jax.experimental import pallas as pl
from jax.experimental.pallas import tpu as pltpu
from jax.sharding import PartitionSpec as P

MESH = pl.DeviceIdType.MESH
D = 1152
ROWS = 72
TOKENS = 256
COLS = 64
NZ = 16
TILES = 9
LANES = 128
LAG = 1
QO_START = 1
QO_LAG = 2
LOWEST = -3.0e38
EPS = 1e-06


def kernel(
    tok_hbm, qkv_ref, ow_ref, conv_ref, gain_ref, out_ref,
    wkv, wqo, wo, wo_flat, tok_ref, tsib, split, acc, kvb, qb, stage, halo, local,
    part_low, a_in, f_sum, b_in, chip_low, c_in, c_out, readout, mix,
    zkv_s, zkv_r, zqo_s, zqo_r, kvs_s, kvs_r, qos_s, qos_r, load_sem,
    tok_sem, kv_sem, q_sem, o_sem, halo_s, halo_r, a_s, a_r, b_s, b_r, c_s, c_r,
):
    tm = lax.axis_index("tm")
    z = lax.axis_index("space")
    core = lax.rem(tm, 2)
    chip = tm // 2
    x = chip // 4
    y = lax.rem(chip, 4)

    def at(px, py, pc, pz):
        return ((px * 4 + py) * 2 + pc, pz)

    def x_off(i):
        return at(lax.rem(x + i + 4, 4), y, core, z)

    def y_off(i):
        return at(x, lax.rem(y + i + 4, 4), core, z)

    def z_off(i):
        return at(x, y, core, lax.rem(z + i + NZ, NZ))

    sibling = at(x, y, 1 - core, z)

    def remote(src, dst, ssem, rsem, device):
        return pltpu.make_async_remote_copy(
            src_ref=src, dst_ref=dst, send_sem=ssem, recv_sem=rsem,
            device_id=device, device_id_type=MESH,
        )

    slot_tile = [0, 1 + x, 5 + y]
    slot_tile += [1 + lax.rem(x + i, 4) for i in (1, 2, 3)]
    slot_tile += [5 + lax.rem(y + i, 4) for i in (1, 2, 3)]

    def lanes(slot):
        return pl.ds(slot * LANES, LANES)

    def tile_lanes(tile):
        return pl.ds(pl.multiple_of(tile * LANES, LANES), LANES)

    peers = [z_off(1), z_off(-1), z_off(2), z_off(-2), sibling]
    peers += [x_off(i) for i in (1, 2, 3)] + [y_off(i) for i in (1, 2, 3)]
    barrier = pltpu.get_barrier_semaphore()
    for peer in peers:
        pl.semaphore_signal(barrier, inc=1, device_id=peer, device_id_type=MESH)

    def load(slot):
        tile = slot_tile[slot]
        here = wkv.at[z, :, lanes(slot)]
        offset = (1 + core) * TILES + tile
        return pltpu.make_async_copy(qkv_ref.at[:, tile_lanes(offset)], here, load_sem.at[slot])

    def load_qo(slot, origin):
        here = wqo.at[z, :, lanes(slot)]
        source = origin.at[:, tile_lanes(slot_tile[slot])]
        return pltpu.make_async_copy(source, here, load_sem.at[TILES + slot])

    load_tokens = pltpu.make_async_copy(tok_hbm, tok_ref, load_sem.at[2 * TILES])
    for slot in range(TILES):
        load(slot).start()
    load_tokens.start()

    @pl.when(core == 0)
    def _():
        for slot in range(TILES):
            load_qo(slot, qkv_ref).start()

    @pl.when(core == 1)
    def _():
        for slot in range(TILES):
            load_qo(slot, ow_ref).start()

    load_tokens.wait()
    for block in range(NZ):
        split[block, 0:TOKENS, :] = tok_ref[:, block * ROWS : (block + 1) * ROWS]
    for slot in range(TILES):
        load(slot).wait()
        load_qo(slot, ow_ref).wait()

    pl.semaphore_wait(barrier, len(peers))

    def step(way, s):
        span = 2 - lax.rem(s, 2)
        return z_off(span if way == 0 else -span)

    def z_kv(way, s, t, source):
        ref = wkv.at[source, :, lanes(t)]
        return remote(ref, ref, zkv_s.at[way, s - 1, t], zkv_r.at[way, s - 1, t], step(way, s))

    def z_qo(way, s, source):
        ref = wqo.at[source, :, pl.ds(0, 3 * LANES)]
        return remote(ref, ref, zqo_s.at[way, s - 1], zqo_r.at[way, s - 1], step(way, s))

    def share(buf, ssem, rsem, way, s, source, line, i):
        device = x_off(-i) if line == 0 else y_off(-i)
        at_sem = (way, s - 1, 3 * line + i - 1)
        return remote(
            buf.at[source, :, lanes(1 + line)], buf.at[source, :, lanes(2 + 3 * line + i)],
            ssem.at[at_sem], rsem.at[at_sem], device,
        )

    def source_of(way, s):
        return lax.rem(z + NZ - s, NZ) if way == 0 else lax.rem(z + s, NZ)

    for t in (1, 2, 0):
        for way in range(2):
            z_kv(way, 2, t, z).start()
    for t in (1, 2, 0):
        for way in range(2):
            z_kv(way, 1, t, z).start()
    token_swap = remote(tok_ref, tsib, tok_sem.at[0], tok_sem.at[1], sibling)
    token_swap.start()
    token_swap.wait()
    for block in range(NZ):
        split[block, TOKENS : 2 * TOKENS, :] = tsib[:, block * ROWS : (block + 1) * ROWS]

    def add_source(buf, source, first):
        left = split[source]
        for n in range(3):
            cols = pl.ds(n * 3 * LANES, 3 * LANES)
            term = jnp.dot(left, buf[source, :, cols], preferred_element_type=jnp.float32)
            acc[:, cols] = term if first else acc[:, cols] + term

    add_source(wkv, z, True)

    def pass_kv(way, s, source, onward):
        for t in (1, 2, 0):
            z_kv(way, s, t, source).wait_recv()
            if onward:
                for nxt in (2, 1):
                    @pl.when(s + nxt <= 8 - way)
                    def _():
                        z_kv(way, s + nxt, t, source).start()

        for line in range(2):
            for i in (1, 2, 3):
                share(wkv, kvs_s, kvs_r, way, s, source, line, i).start()

    def pass_qo(way, s, source, onward):
        z_qo(way, s, source).wait_recv()
        if onward:
            for nxt in (2, 1):
                @pl.when(s + nxt <= 8 - way)
                def _():
                    z_qo(way, s + nxt, source).start()
        for line in range(2):
            for i in (1, 2, 3):
                share(wqo, qos_s, qos_r, way, s, source, line, i).start()

    def take_kv(way, s, source):
        for line in range(2):
            for i in (1, 2, 3):
                share(wkv, kvs_s, kvs_r, way, s, source, line, i).wait_recv()
        add_source(wkv, source, False)

    def at_place(m, job):
        for odd in range(2):
            s = 2 * m - odd
            for way in range(2):
                @pl.when((m >= 1) & (s <= 8 - way))
                def _():
                    job(way, s, source_of(way, s), odd == 0)

    def ring(m, carry):
        @pl.when(m <= 4)
        def _():
            at_place(m, pass_kv)

        @pl.when(m == QO_START)
        def _():
            for nxt in (2, 1):
                for way in range(2):
                    z_qo(way, nxt, z).start()

        @pl.when(m > QO_LAG)
        def _():
            at_place(m - QO_LAG, pass_qo)

        @pl.when((m > LAG) & (m <= 4 + LAG))
        def _():
            at_place(m - LAG, lambda way, s, source, _: take_kv(way, s, source))

        return carry

    lax.fori_loop(1, 5 + QO_LAG, ring, 0)

    floor = jnp.where(core == 0, 0.0, LOWEST).astype(jnp.float32)
    swaps = []
    for n in range(3):
        for k in range(3):
            slot = 3 * n + k
            stage[n, :, lanes(k)] = jnp.maximum(acc[TOKENS:, lanes(slot)], floor).astype(jnp.bfloat16)
        swap = remote(stage.at[n], stage.at[3 + n], kv_sem.at[n], kv_sem.at[3 + n], sibling)
        swap.start()
        swaps.append(swap)
    for slot in range(TILES):
        kvb[core, :, tile_lanes(slot_tile[slot])] = jnp.maximum(
            acc[0:TOKENS, lanes(slot)], floor
        ).astype(jnp.bfloat16)
    for n in range(3):
        swaps[n].wait()
        for k in range(3):
            slot = 3 * n + k
            kvb[1 - core, :, tile_lanes(slot_tile[slot])] = stage[3 + n, :, lanes(k)]

    down = remote(kvb.at[1, pl.ds(3 * COLS, COLS)], halo.at[0], halo_s.at[0], halo_r.at[0], z_off(1))
    up = remote(kvb.at[1, pl.ds(0, COLS)], halo.at[1], halo_s.at[1], halo_r.at[1], z_off(-1))

    row_head = lax.broadcasted_iota(jnp.int32, (LANES, LANES), 0) // 32
    col_head = lax.broadcasted_iota(jnp.int32, (LANES, LANES), 1) // 32
    same_head = row_head == col_head

    mine = z * 2 + core

    def a_copy(h):
        return remote(
            part_low.at[h], a_in.at[core * NZ + z], a_s.at[h], a_r.at[core * NZ + z],
            at(x, y, h % 2, h // 2),
        )

    for j in range(TILES):
        gram = lax.dot_general(
            kvb[0, :, lanes(j)], kvb[1, :, lanes(j)], (((0,), (0,)), ((), ())),
            preferred_element_type=jnp.float32,
        )
        gram = jnp.where(same_head, gram, 0.0)
        part = gram[0:32] + gram[32:64] + gram[64:96] + gram[96:128]
        part_low[2 * j] = part[0:16].astype(jnp.bfloat16)
        part_low[2 * j + 1] = part[16:32].astype(jnp.bfloat16)
        for h in (2 * j, 2 * j + 1):
            @pl.when(mine != h)
            def _():
                a_copy(h).start()

    @pl.when(z < NZ - 1)
    def _():
        down.start()

    @pl.when(z > 0)
    def _():
        up.start()

    def wait_shares(s, carry):
        for way in range(2):
            @pl.when(s <= 8 - way)
            def _():
                source = source_of(way, s)
                for line in range(2):
                    for i in (1, 2, 3):
                        share(wqo, qos_s, qos_r, way, s, source, line, i).wait_recv()
        return carry

    lax.fori_loop(1, 9, wait_shares, 0)

    o_send = remote(wqo, wo, o_sem.at[0], o_sem.at[1], sibling)
    q_send = remote(qb.at[1], qb.at[0], q_sem.at[0], q_sem.at[1], sibling)

    @pl.when(core == 1)
    def _():
        o_send.start()

    @pl.when(core == 0)
    def _():
        add_source(wqo, 0, True)

        def more(source, carry):
            add_source(wqo, source, False)
            return carry

        lax.fori_loop(1, NZ, more, 0)
        for slot in range(TILES):
            qb[1, :, tile_lanes(slot_tile[slot])] = jnp.maximum(
                acc[TOKENS:, lanes(slot)], 0.0
            ).astype(jnp.bfloat16)
        q_send.start()
        for slot in range(TILES):
            qb[0, :, tile_lanes(slot_tile[slot])] = jnp.maximum(
                acc[0:TOKENS, lanes(slot)], 0.0
            ).astype(jnp.bfloat16)

    def b_copy(i):
        later = chip + i
        return remote(
            chip_low, b_in.at[i - 1], b_s.at[i - 1], b_r.at[i - 1], (later * 2 + core, z)
        )

    def c_copy(pc, k):
        return remote(
            c_out.at[pc], c_in.at[mine], c_s.at[pc * NZ + k], c_r.at[mine],
            at(x, y, pc, lax.rem(z + k, NZ)),
        )

    far_first = (8, 7, 9, 6, 10, 5, 11, 4, 12, 3, 13, 2, 14, 1, 15)

    @pl.when(z < TILES)
    def _():
        a_in[core * NZ + z] = part_low[mine]
        for pc in range(2):
            f_sum[pc] = jnp.zeros((16, LANES), jnp.float32)

            def gather(k, carry):
                source = pc * NZ + lax.rem(z + k, NZ)

                @pl.when(source != core * NZ + z)
                def _():
                    remote(
                        part_low.at[0], a_in.at[source], a_s.at[0], a_r.at[source], sibling
                    ).wait_recv()

                f_sum[pc] = f_sum[pc] + a_in[source].astype(jnp.float32)
                return carry

            lax.fori_loop(0, NZ, gather, 0)
        chip_low[...] = (f_sum[0] + f_sum[1]).astype(jnp.bfloat16)
        for i in range(NZ - 1, 0, -1):
            @pl.when(chip + i < NZ)
            def _():
                b_copy(i).start()
        for i in range(1, NZ):
            @pl.when(chip >= i)
            def _():
                b_copy(i).wait_recv()
                f_sum[0] = f_sum[0] + b_in[i - 1].astype(jnp.float32)
        c_out[0] = f_sum[0].astype(jnp.bfloat16)
        c_out[1] = (f_sum[0] + f_sum[1]).astype(jnp.bfloat16)
        c_in[mine] = c_out[core]
        for k in far_first:
            for pc in range(2):
                c_copy(pc, k).start()
        for pc in range(2):
            @pl.when(core != pc)
            def _():
                c_copy(pc, 0).start()

    @pl.when(z > 0)
    def _():
        down.wait_recv()

    @pl.when(z == 0)
    def _():
        halo[0] = jnp.zeros((COLS, D), jnp.bfloat16)

    @pl.when(z < NZ - 1)
    def _():
        up.wait_recv()

    @pl.when(z == NZ - 1)
    def _():
        halo[1] = jnp.zeros((COLS, D), jnp.bfloat16)

    col = lax.broadcasted_iota(jnp.int32, (COLS, LANES), 0)

    def conv(j, carry):
        cols = tile_lanes(j)
        weight = [conv_ref[a, :, cols] for a in range(3)]
        sums = [jnp.zeros((COLS, LANES), jnp.float32) for _ in range(4)]
        for row in range(6):
            if row == 0:
                mid = halo[0, :, cols]
            elif row == 5:
                mid = halo[1, :, cols]
            else:
                mid = kvb[1, pl.ds((row - 1) * COLS, COLS), cols]
            mid = mid.astype(jnp.float32)
            left = jnp.where(col == 0, 0.0, pltpu.roll(mid, 1, 0))
            right = jnp.where(col == COLS - 1, 0.0, pltpu.roll(mid, COLS - 1, 0))
            for a in range(3):
                r = row - a
                if 0 <= r < 4:
                    sums[r] = (
                        sums[r] + weight[a][0:1] * left + weight[a][1:2] * mid
                        + weight[a][2:3] * right
                    )
        for r in range(4):
            local[pl.ds(r * COLS, COLS), cols] = sums[r]
        return carry

    lax.fori_loop(0, TILES, conv, 0)

    @pl.when(core == 0)
    def _():
        o_send.wait_recv()

    def flatten(buf):
        def pair(k, carry):
            for slot in range(TILES):
                both = jnp.concatenate(
                    [
                        buf[2 * k, :, lanes(slot)].astype(jnp.float32),
                        buf[2 * k + 1, :, lanes(slot)].astype(jnp.float32),
                    ],
                    axis=0,
                )
                rows = pl.ds(pl.multiple_of(k * 2 * ROWS, 16), 2 * ROWS)
                wo_flat[rows, lanes(slot)] = both.astype(jnp.bfloat16)
            return carry

        lax.fori_loop(0, NZ // 2, pair, 0)

    @pl.when(core == 0)
    def _():
        flatten(wo)

    @pl.when(core == 1)
    def _():
        flatten(wqo)
        q_send.wait_recv()

    for h in range(2 * TILES):
        @pl.when(mine != h)
        def _():
            remote(c_in.at[h], c_in.at[h], c_s.at[0], c_r.at[h], sibling).wait_recv()

    square = jnp.zeros((TOKENS, LANES), jnp.float32)
    for j in range(TILES):
        halves = [c_in[2 * j].astype(jnp.float32), c_in[2 * j + 1].astype(jnp.float32)]
        state = jnp.concatenate(halves * 4, axis=0)
        state = jnp.where(same_head, state, 0.0).astype(jnp.bfloat16)
        term = jnp.dot(qb[0, :, lanes(j)], state, preferred_element_type=jnp.float32)
        readout[:, lanes(j)] = term
        square = square + term * term
    mean_square = jnp.sum(square, axis=-1, keepdims=True) * (1.0 / D)
    scale = lax.rsqrt(mean_square + EPS)
    for j in range(TILES):
        normed = readout[:, lanes(j)] * scale * gain_ref[:, lanes(j)]
        mix[:, lanes(j)] = (normed + local[:, lanes(j)]).astype(jnp.bfloat16)
    for n in range(3):
        cols = pl.ds(n * 3 * LANES, 3 * LANES)
        result = jnp.dot(mix[...], wo_flat[:, cols], preferred_element_type=jnp.float32)
        result = result.astype(jnp.bfloat16)
        for k in range(3):
            out_ref[:, tile_lanes(slot_tile[3 * n + k])] = result[:, k * LANES : (k + 1) * LANES]

    def sends(s, carry):
        for way in range(2):
            @pl.when(s <= 8 - way)
            def _():
                source = source_of(way, s)
                for t in range(3):
                    z_kv(way, s, t, source).wait_send()
                z_qo(way, s, source).wait_send()
                for line in range(2):
                    for i in (1, 2, 3):
                        share(wkv, kvs_s, kvs_r, way, s, source, line, i).wait_send()
                        share(wqo, qos_s, qos_r, way, s, source, line, i).wait_send()
        return carry

    lax.fori_loop(1, 9, sends, 0)
    for h in range(2 * TILES):
        @pl.when(mine != h)
        def _():
            a_copy(h).wait_send()

    @pl.when(z < NZ - 1)
    def _():
        down.wait_send()

    @pl.when(z > 0)
    def _():
        up.wait_send()

    @pl.when(core == 1)
    def _():
        o_send.wait_send()

    @pl.when(core == 0)
    def _():
        q_send.wait_send()

    @pl.when(z < TILES)
    def _():
        for i in range(1, NZ):
            @pl.when(chip + i < NZ)
            def _():
                b_copy(i).wait_send()
        for k in far_first:
            for pc in range(2):
                c_copy(pc, k).wait_send()
        for pc in range(2):
            @pl.when(core != pc)
            def _():
                c_copy(pc, 0).wait_send()


def per_device(video_tokens, qkv_weight, out_weight, conv_weight, norm_gain):
    tokens = video_tokens.reshape(TOKENS, D)
    bf16, f32 = jnp.bfloat16, jnp.float32
    vmem = pl.BlockSpec(memory_space=pltpu.VMEM)
    hbm = pl.BlockSpec(memory_space=pltpu.HBM)
    dma = pltpu.SemaphoreType.DMA
    result = pl.pallas_call(
        kernel,
        out_shape=jax.ShapeDtypeStruct((TOKENS, D), bf16),
        in_specs=[hbm] * 3 + [vmem] * 2,
        out_specs=vmem,
        scratch_shapes=[
            pltpu.VMEM((NZ, ROWS, D), bf16),
            pltpu.VMEM((NZ, ROWS, D), bf16),
            pltpu.VMEM((NZ, ROWS, D), bf16),
            pltpu.VMEM((D, D), bf16),
            pltpu.VMEM((TOKENS, D), bf16),
            pltpu.VMEM((TOKENS, D), bf16),
            pltpu.VMEM((NZ, 2 * TOKENS, ROWS), bf16),
            pltpu.VMEM((2 * TOKENS, D), f32),
            pltpu.VMEM((2, TOKENS, D), bf16),
            pltpu.VMEM((2, TOKENS, D), bf16),
            pltpu.VMEM((6, TOKENS, 3 * LANES), bf16),
            pltpu.VMEM((2, COLS, D), bf16),
            pltpu.VMEM((TOKENS, D), f32),
            pltpu.VMEM((2 * TILES, 16, LANES), bf16),
            pltpu.VMEM((2 * NZ, 16, LANES), bf16),
            pltpu.VMEM((2, 16, LANES), f32),
            pltpu.VMEM((NZ - 1, 16, LANES), bf16),
            pltpu.VMEM((16, LANES), bf16),
            pltpu.VMEM((2 * TILES, 16, LANES), bf16),
            pltpu.VMEM((2, 16, LANES), bf16),
            pltpu.VMEM((TOKENS, D), f32),
            pltpu.VMEM((TOKENS, D), bf16),
            dma((2, 8, 3)), dma((2, 8, 3)),
            dma((2, 8)), dma((2, 8)),
            dma((2, 8, 6)), dma((2, 8, 6)),
            dma((2, 8, 6)), dma((2, 8, 6)),
            dma((2 * TILES + 1,)),
            dma((2,)),
            dma((6,)),
            dma((2,)),
            dma((2,)),
            dma((2,)), dma((2,)),
            dma((2 * TILES,)), dma((2 * NZ,)),
            dma((NZ - 1,)), dma((NZ - 1,)),
            dma((2 * NZ,)), dma((2 * TILES,)),
        ],
        compiler_params=pltpu.CompilerParams(
            collective_id=0, has_side_effects=True, vmem_limit_bytes=48 * 2**20
        ),
        name="block",
    )(tokens, qkv_weight, out_weight, conv_weight, norm_gain.reshape(1, D))
    return result.reshape(video_tokens.shape)


def solution(mesh):
    in_specs = (P("tm", "space", None, None), P("space", None), P("space", None), P(), P())
    out_specs = P("tm", "space", None, None)
    return jax.shard_map(
        per_device, mesh=mesh, in_specs=in_specs, out_specs=out_specs, check_vma=False
    )
```

```python
import jax
import jax.numpy as jnp
from jax import lax
from jax.experimental import pallas as pl
from jax.experimental.pallas import tpu as pltpu
from jax.sharding import PartitionSpec as P

MESH = pl.DeviceIdType.MESH
D = 1152
ROWS = 72
TOKENS = 256
COLS = 64
NZ = 16
TILES = 9
LANES = 128
QO_START = 2
QO_FIRST = 4
P2 = 0
P3 = 1
P4 = 2
T1 = 3
T2 = 4
LOWEST = -3.0e38
EPS = 1e-06


def kernel(
    tok_hbm, qkv_ref, ow_ref, conv_hbm, gain_ref, out_ref,
    wkv, wqo, wo, wo_flat, conv_ref, tok_ref, tsib, split, acc, kvb, qb, stage, halo, local,
    part_low, a_in, f_sum, b_in, chip_low, c_in, c_out, readout, mix,
    zkv_r, zqo_r, kvs_r, qos_r, kv_s, qo_s, load_sem,
    tok_sem, kv_sem, q_sem, o_sem, halo_s, halo_r, a_s, a_r, b_s, b_r, c_s, c_r,
):
    tm = lax.axis_index("tm")
    z = lax.axis_index("space")
    core = lax.rem(tm, 2)
    chip = tm // 2
    x = chip // 4
    y = lax.rem(chip, 4)

    def at(px, py, pc, pz):
        return ((px * 4 + py) * 2 + pc, pz)

    def x_off(i):
        return at(lax.rem(x + i + 4, 4), y, core, z)

    def y_off(i):
        return at(x, lax.rem(y + i + 4, 4), core, z)

    def z_off(i):
        return at(x, y, core, lax.rem(z + i + NZ, NZ))

    sibling = at(x, y, 1 - core, z)

    def remote(src, dst, ssem, rsem, device):
        return pltpu.make_async_remote_copy(
            src_ref=src, dst_ref=dst, send_sem=ssem, recv_sem=rsem,
            device_id=device, device_id_type=MESH,
        )

    slot_tile = [0, 1 + x, 5 + y]
    slot_tile += [1 + lax.rem(x + i, 4) for i in (1, 2, 3)]
    slot_tile += [5 + lax.rem(y + i, 4) for i in (1, 2, 3)]

    def lanes(slot):
        return pl.ds(slot * LANES, LANES)

    def tile_lanes(tile):
        return pl.ds(pl.multiple_of(tile * LANES, LANES), LANES)

    peers = [z_off(1), z_off(-1), z_off(2), z_off(-2), sibling]
    peers += [x_off(i) for i in (1, 2, 3)] + [y_off(i) for i in (1, 2, 3)]
    barrier = pltpu.get_barrier_semaphore()
    for peer in peers:
        pl.semaphore_signal(barrier, inc=1, device_id=peer, device_id_type=MESH)

    def load(slot):
        tile = slot_tile[slot]
        here = wkv.at[z, :, lanes(slot)]
        offset = (1 + core) * TILES + tile
        return pltpu.make_async_copy(qkv_ref.at[:, tile_lanes(offset)], here, load_sem.at[0])

    def load_qo(slot, origin):
        here = wqo.at[z, :, lanes(slot)]
        source = origin.at[:, tile_lanes(slot_tile[slot])]
        return pltpu.make_async_copy(source, here, load_sem.at[1])

    load_tokens = pltpu.make_async_copy(tok_hbm, tok_ref, load_sem.at[2])
    for slot in range(TILES):
        load(slot).start()
    load_tokens.start()

    @pl.when(core == 0)
    def _():
        for slot in range(TILES):
            load_qo(slot, qkv_ref).start()

    @pl.when(core == 1)
    def _():
        for slot in range(TILES):
            load_qo(slot, ow_ref).start()

    load_conv = pltpu.make_async_copy(conv_hbm, conv_ref, load_sem.at[3])
    load_conv.start()

    def local_wait(ref, sem):
        pltpu.make_async_copy(ref, ref, sem).wait()

    local_wait(wkv.at[z], load_sem.at[0])
    load_tokens.wait()
    pl.semaphore_wait(barrier, len(peers))

    def step(way, s):
        span = 2 - lax.rem(s, 2)
        return z_off(span if way == 0 else -span)

    def z_kv(way, s, t, source):
        ref = wkv.at[source, :, lanes(t)]
        return remote(ref, ref, kv_s.at[0], zkv_r.at[way, s - 1, t], step(way, s))

    def z_qo(way, s, source):
        ref = wqo.at[source, :, pl.ds(0, 3 * LANES)]
        return remote(ref, ref, qo_s.at[0], zqo_r.at[way, s - 1], step(way, s))

    def share(buf, ssem, rsem, source, line, i):
        return remote(
            buf.at[source, :, lanes(1 + line)], buf.at[source, :, lanes(2 + 3 * line + i)],
            ssem, rsem, x_off(-i) if line == 0 else y_off(-i),
        )

    def share_all(buf, ssem, rsem, source):
        for i in (2, 1, 3):
            for line in range(2):
                share(buf, ssem, rsem, source, line, i).start()

    def source_of(way, s):
        return lax.rem(z + NZ - s, NZ) if way == 0 else lax.rem(z + s, NZ)

    for s in (2, 1):
        for t in (1, 2, 0):
            for way in range(2):
                z_kv(way, s, t, z).start()
    token_swap = remote(tok_ref, tsib, tok_sem.at[0], tok_sem.at[1], sibling)
    token_swap.start()
    for block in range(NZ):
        split[block, 0:TOKENS, :] = tok_ref[:, block * ROWS : (block + 1) * ROWS]
    token_swap.wait()
    for block in range(NZ):
        split[block, TOKENS : 2 * TOKENS, :] = tsib[:, block * ROWS : (block + 1) * ROWS]

    def add_source(buf, source, first):
        left = split[source]
        for n in range(3):
            cols = pl.ds(n * 3 * LANES, 3 * LANES)
            term = jnp.dot(left, buf[source, :, cols], preferred_element_type=jnp.float32)
            acc[:, cols] = term if first else acc[:, cols] + term

    add_source(wkv, z, True)

    def pass_kv(m):
        s = 2 * m
        for t in (1, 2, 0):
            for way in range(2):
                @pl.when(s <= 8 - way)
                def _():
                    z_kv(way, s, t, source_of(way, s)).wait_recv()

                @pl.when(s + 2 <= 8 - way)
                def _():
                    z_kv(way, s + 2, t, source_of(way, s)).start()

        for t in (1, 2, 0):
            for way in range(2):
                @pl.when(s + 1 <= 8 - way)
                def _():
                    z_kv(way, s + 1, t, source_of(way, s)).start()

        for odd in range(2):
            for way in range(2):
                @pl.when(s - odd <= 8 - way)
                def _():
                    source = source_of(way, s - odd)
                    if odd:
                        for t in (1, 2, 0):
                            z_kv(way, s - 1, t, source).wait_recv()
                    share_all(wkv, kv_s.at[0], kvs_r.at[way, s - odd - 1], source)

    def take_kv(m):
        for odd in (1, 0):
            s = 2 * m - odd
            for way in range(2):
                @pl.when(s <= 8 - way)
                def _():
                    source = source_of(way, s)
                    shared = wkv.at[source, :, pl.ds(3 * LANES, 6 * LANES)]
                    remote(shared, shared, kv_s.at[0], kvs_r.at[way, s - 1], sibling).wait_recv()
                    add_source(wkv, source, False)

    def start_qo():
        local_wait(wqo.at[z], load_sem.at[1])
        for s in (2, 1):
            for way in range(2):
                z_qo(way, s, z).start()

    def pass_qo(m):
        for odd in range(2):
            s = 2 * m - odd
            for way in range(2):
                @pl.when(s <= 8 - way)
                def _():
                    source = source_of(way, s)
                    z_qo(way, s, source).wait_recv()
                    if odd == 0:
                        for nxt in (2, 1):
                            @pl.when(s + nxt <= 8 - way)
                            def _():
                                z_qo(way, s + nxt, source).start()

                    share_all(wqo, qo_s.at[0], qos_r.at[m - 1], source)

    def ring(m, carry):
        @pl.when(m <= 4)
        def _():
            pass_kv(m)

        @pl.when(m == QO_START)
        def _():
            start_qo()

        @pl.when(m == QO_FIRST)
        def _():
            pass_qo(1)

        @pl.when(m > 1)
        def _():
            take_kv(m - 1)

        return carry

    def o_copy(source):
        return remote(wqo.at[source], wo.at[source], o_sem.at[0], o_sem.at[1], sibling)

    q_send = remote(qb.at[1], qb.at[0], q_sem.at[0], q_sem.at[1], sibling)

    def use_qo(source, first):
        @pl.when(core == 0)
        def _():
            add_source(wqo, source, first)

        @pl.when(core == 1)
        def _():
            o_copy(source).start()

    def take_qo(m):
        shared = wqo.at[0 : (3 if m == 4 else 4), :, pl.ds(0, 6 * LANES)]
        remote(shared, shared, qo_s.at[0], qos_r.at[m - 1], sibling).wait_recv()

        def one(k, carry):
            s = 2 * m - k // 2
            source = jnp.where(lax.rem(k, 2) == 0, source_of(0, s), source_of(1, s))

            @pl.when((lax.rem(k, 2) == 0) | (s <= 7))
            def _():
                use_qo(source, False)

            return carry

        lax.fori_loop(0, 4, one, 0)

    def hook(place):
        for m, passed in ((2, P2), (3, P3), (4, P4)):
            if passed == place:
                pass_qo(m)
        for m, taken in ((1, T1), (2, T2)):
            if taken == place:
                if m == 1:
                    use_qo(z, True)
                take_qo(m)

    lax.fori_loop(1, 6, ring, 0)
    hook(0)

    floor = jnp.where(core == 0, 0.0, LOWEST).astype(jnp.float32)
    swaps = []
    for n in range(3):
        for k in range(3):
            slot = 3 * n + k
            stage[n, :, lanes(k)] = jnp.maximum(acc[TOKENS:, lanes(slot)], floor).astype(jnp.bfloat16)
        swap = remote(stage.at[n], stage.at[3 + n], kv_sem.at[n], kv_sem.at[3 + n], sibling)
        swap.start()
        swaps.append(swap)
    for slot in range(TILES):
        kvb[core, :, tile_lanes(slot_tile[slot])] = jnp.maximum(
            acc[0:TOKENS, lanes(slot)], floor
        ).astype(jnp.bfloat16)
    for n in range(3):
        swaps[n].wait()
        for k in range(3):
            slot = 3 * n + k
            kvb[1 - core, :, tile_lanes(slot_tile[slot])] = stage[3 + n, :, lanes(k)]

    down = remote(kvb.at[1, pl.ds(3 * COLS, COLS)], halo.at[0], halo_s.at[0], halo_r.at[0], z_off(1))
    up = remote(kvb.at[1, pl.ds(0, COLS)], halo.at[1], halo_s.at[1], halo_r.at[1], z_off(-1))

    row_head = lax.broadcasted_iota(jnp.int32, (LANES, LANES), 0) // 32
    col_head = lax.broadcasted_iota(jnp.int32, (LANES, LANES), 1) // 32
    same_head = row_head == col_head

    mine = z * 2 + core

    def a_copy(h):
        return remote(
            part_low.at[h], a_in.at[core * NZ + z], a_s.at[0], a_r.at[0],
            at(x, y, h % 2, h // 2),
        )

    for j in range(TILES):
        gram = lax.dot_general(
            kvb[0, :, lanes(j)], kvb[1, :, lanes(j)], (((0,), (0,)), ((), ())),
            preferred_element_type=jnp.float32,
        )
        gram = jnp.where(same_head, gram, 0.0)
        part = gram[0:32] + gram[32:64] + gram[64:96] + gram[96:128]
        part_low[2 * j] = part[0:16].astype(jnp.bfloat16)
        part_low[2 * j + 1] = part[16:32].astype(jnp.bfloat16)
        for h in (2 * j, 2 * j + 1):
            @pl.when(mine != h)
            def _():
                a_copy(h).start()

    @pl.when(z < NZ - 1)
    def _():
        down.start()

    @pl.when(z > 0)
    def _():
        up.start()

    hook(1)

    @pl.when(z > 0)
    def _():
        down.wait_recv()

    @pl.when(z == 0)
    def _():
        halo[0] = jnp.zeros((COLS, D), jnp.bfloat16)

    @pl.when(z < NZ - 1)
    def _():
        up.wait_recv()

    @pl.when(z == NZ - 1)
    def _():
        halo[1] = jnp.zeros((COLS, D), jnp.bfloat16)

    load_conv.wait()
    col = lax.broadcasted_iota(jnp.int32, (COLS, LANES), 0)

    def conv(j, carry):
        cols = tile_lanes(j)
        weight = [conv_ref[a, :, cols] for a in range(3)]
        sums = [jnp.zeros((COLS, LANES), jnp.float32) for _ in range(4)]
        for row in range(6):
            if row == 0:
                mid = halo[0, :, cols]
            elif row == 5:
                mid = halo[1, :, cols]
            else:
                mid = kvb[1, pl.ds((row - 1) * COLS, COLS), cols]
            mid = mid.astype(jnp.float32)
            left = jnp.where(col == 0, 0.0, pltpu.roll(mid, 1, 0))
            right = jnp.where(col == COLS - 1, 0.0, pltpu.roll(mid, COLS - 1, 0))
            for a in range(3):
                r = row - a
                if 0 <= r < 4:
                    sums[r] = (
                        sums[r] + weight[a][0:1] * left + weight[a][1:2] * mid
                        + weight[a][2:3] * right
                    )
        for r in range(4):
            local[pl.ds(r * COLS, COLS), cols] = sums[r]
        return carry

    lax.fori_loop(0, TILES, conv, 0)

    hook(2)

    def b_copy(i):
        later = chip + i
        return remote(chip_low, b_in.at[i - 1], b_s.at[0], b_r.at[0], (later * 2 + core, z))

    def c_copy(pc, k):
        return remote(
            c_out.at[pc], c_in.at[mine], c_s.at[0], c_r.at[0], at(x, y, pc, lax.rem(z + k, NZ))
        )

    far_first = (8, 7, 9, 6, 10, 5, 11, 4, 12, 3, 13, 2, 14, 1, 15)

    @pl.when(z < TILES)
    def _():
        a_in[core * NZ + z] = part_low[mine]
        others = a_in.at[0 : 2 * NZ - 1]
        remote(others, others, a_s.at[0], a_r.at[0], sibling).wait_recv()
        for pc in range(2):
            f_sum[pc] = jnp.sum(a_in[pc * NZ : (pc + 1) * NZ].astype(jnp.float32), axis=0)
        chip_low[...] = (f_sum[0] + f_sum[1]).astype(jnp.bfloat16)
        for i in range(NZ - 1, 0, -1):
            @pl.when(chip + i < NZ)
            def _():
                b_copy(i).start()

    hook(3)

    @pl.when(z < TILES)
    def _():
        for n in range(1, NZ):
            @pl.when(chip == n)
            def _():
                earlier = b_in.at[0:n]
                remote(earlier, earlier, b_s.at[0], b_r.at[0], sibling).wait_recv()
                f_sum[0] = f_sum[0] + jnp.sum(b_in[0:n].astype(jnp.float32), axis=0)

        c_out[0] = f_sum[0].astype(jnp.bfloat16)
        c_out[1] = (f_sum[0] + f_sum[1]).astype(jnp.bfloat16)
        c_in[mine] = c_out[core]
        for k in far_first:
            for pc in range(2):
                c_copy(pc, k).start()
        for pc in range(2):
            @pl.when(core != pc)
            def _():
                c_copy(pc, 0).start()

    hook(4)
    take_qo(3)
    take_qo(4)

    @pl.when(core == 0)
    def _():
        for slot in range(TILES):
            qb[1, :, tile_lanes(slot_tile[slot])] = jnp.maximum(
                acc[TOKENS:, lanes(slot)], 0.0
            ).astype(jnp.bfloat16)
        q_send.start()
        for slot in range(TILES):
            qb[0, :, tile_lanes(slot_tile[slot])] = jnp.maximum(
                acc[0:TOKENS, lanes(slot)], 0.0
            ).astype(jnp.bfloat16)

    @pl.when(core == 0)
    def _():
        remote(wo, wo, o_sem.at[0], o_sem.at[1], sibling).wait_recv()

    def flatten(buf):
        def pair(k, carry):
            for slot in range(TILES):
                both = jnp.concatenate(
                    [
                        buf[2 * k, :, lanes(slot)].astype(jnp.float32),
                        buf[2 * k + 1, :, lanes(slot)].astype(jnp.float32),
                    ],
                    axis=0,
                )
                rows = pl.ds(pl.multiple_of(k * 2 * ROWS, 16), 2 * ROWS)
                wo_flat[rows, lanes(slot)] = both.astype(jnp.bfloat16)
            return carry

        lax.fori_loop(0, NZ // 2, pair, 0)

    @pl.when(core == 0)
    def _():
        flatten(wo)

    @pl.when(core == 1)
    def _():
        flatten(wqo)
        q_send.wait_recv()

    owner = z < TILES

    def wait_c(count):
        rest = c_in.at[0:count]
        remote(rest, rest, c_s.at[0], c_r.at[0], sibling).wait_recv()

    @pl.when(owner)
    def _():
        wait_c(2 * TILES - 1)

    @pl.when(jnp.logical_not(owner))
    def _():
        wait_c(2 * TILES)

    square = jnp.zeros((TOKENS, LANES), jnp.float32)
    for j in range(TILES):
        halves = [c_in[2 * j].astype(jnp.float32), c_in[2 * j + 1].astype(jnp.float32)]
        state = jnp.concatenate(halves * 4, axis=0)
        state = jnp.where(same_head, state, 0.0).astype(jnp.bfloat16)
        term = jnp.dot(qb[0, :, lanes(j)], state, preferred_element_type=jnp.float32)
        readout[:, lanes(j)] = term
        square = square + term * term
    mean_square = jnp.sum(square, axis=-1, keepdims=True) * (1.0 / D)
    scale = lax.rsqrt(mean_square + EPS)
    for j in range(TILES):
        normed = readout[:, lanes(j)] * scale * gain_ref[lanes(j)].reshape(1, LANES)
        mix[:, lanes(j)] = (normed + local[:, lanes(j)]).astype(jnp.bfloat16)
    for n in range(3):
        cols = pl.ds(n * 3 * LANES, 3 * LANES)
        result = jnp.dot(mix[...], wo_flat[:, cols], preferred_element_type=jnp.float32)
        result = result.astype(jnp.bfloat16)
        for k in range(3):
            out_ref[:, tile_lanes(slot_tile[3 * n + k])] = result[:, k * LANES : (k + 1) * LANES]

    def sent(ref, sem):
        remote(ref, ref, sem, sem, sibling).wait_send()

    sent(wkv.at[0:15], kv_s.at[0])
    sent(wqo.at[0:15], qo_s.at[0])

    @pl.when(owner)
    def _():
        sent(part_low.at[0 : 2 * TILES - 1], a_s.at[0])
        sent(a_in.at[0 : 2 * NZ - 1], c_s.at[0])
        for n in range(1, NZ):
            @pl.when(chip + n == NZ - 1)
            def _():
                sent(b_in.at[0:n], b_s.at[0])

    @pl.when(jnp.logical_not(owner))
    def _():
        sent(part_low, a_s.at[0])

    @pl.when(z < NZ - 1)
    def _():
        down.wait_send()

    @pl.when(z > 0)
    def _():
        up.wait_send()

    @pl.when(core == 1)
    def _():
        sent(wqo, o_sem.at[0])

    @pl.when(core == 0)
    def _():
        q_send.wait_send()


def per_device(video_tokens, qkv_weight, out_weight, conv_weight, norm_gain):
    tokens = video_tokens.reshape(TOKENS, D)
    bf16, f32 = jnp.bfloat16, jnp.float32
    vmem = pl.BlockSpec(memory_space=pltpu.VMEM)
    hbm = pl.BlockSpec(memory_space=pltpu.HBM)
    dma = pltpu.SemaphoreType.DMA
    result = pl.pallas_call(
        kernel,
        out_shape=jax.ShapeDtypeStruct((TOKENS, D), bf16),
        in_specs=[hbm] * 4 + [vmem],
        out_specs=vmem,
        scratch_shapes=[
            pltpu.VMEM((NZ, ROWS, D), bf16),
            pltpu.VMEM((NZ, ROWS, D), bf16),
            pltpu.VMEM((NZ, ROWS, D), bf16),
            pltpu.VMEM((D, D), bf16),
            pltpu.VMEM((3, 3, D), f32),
            pltpu.VMEM((TOKENS, D), bf16),
            pltpu.VMEM((TOKENS, D), bf16),
            pltpu.VMEM((NZ, 2 * TOKENS, ROWS), bf16),
            pltpu.VMEM((2 * TOKENS, D), f32),
            pltpu.VMEM((2, TOKENS, D), bf16),
            pltpu.VMEM((2, TOKENS, D), bf16),
            pltpu.VMEM((6, TOKENS, 3 * LANES), bf16),
            pltpu.VMEM((2, COLS, D), bf16),
            pltpu.VMEM((TOKENS, D), f32),
            pltpu.VMEM((2 * TILES, 16, LANES), bf16),
            pltpu.VMEM((2 * NZ, 16, LANES), bf16),
            pltpu.VMEM((2, 16, LANES), f32),
            pltpu.VMEM((NZ - 1, 16, LANES), bf16),
            pltpu.VMEM((16, LANES), bf16),
            pltpu.VMEM((2 * TILES, 16, LANES), bf16),
            pltpu.VMEM((2, 16, LANES), bf16),
            pltpu.VMEM((TOKENS, D), f32),
            pltpu.VMEM((TOKENS, D), bf16),
            dma((2, 8, 3)), dma((2, 8)), dma((2, 8)), dma((4,)),
            dma((1,)), dma((1,)), dma((4,)),
            dma((2,)), dma((6,)), dma((2,)), dma((2,)),
            dma((2,)), dma((2,)),
            dma((1,)), dma((1,)), dma((1,)), dma((1,)), dma((1,)), dma((1,)),
        ],
        compiler_params=pltpu.CompilerParams(
            collective_id=0, has_side_effects=True, vmem_limit_bytes=63 * 2**20
        ),
        name="block",
    )(tokens, qkv_weight, out_weight, conv_weight, norm_gain)
    return result.reshape(video_tokens.shape)


def solution(mesh):
    in_specs = (P("tm", "space", None, None), P("space", None), P("space", None), P(), P())
    out_specs = P("tm", "space", None, None)
    return jax.shard_map(
        per_device, mesh=mesh, in_specs=in_specs, out_specs=out_specs, check_vma=False
    )
```

```python
import jax
import jax.numpy as jnp
from jax import lax
from jax.experimental import pallas as pl
from jax.experimental.pallas import tpu as pltpu
from jax.sharding import PartitionSpec as P

MESH = pl.DeviceIdType.MESH
D = 1152
ROWS = 72
TOKENS = 256
COLS = 64
NZ = 16
TILES = 9
LANES = 128
QO_START = 2
QO_FIRST = 4
P2 = 0
P3 = 3
P4 = 4
T1 = 4
CONV = 1
T2 = 4
LOWEST = -3.0e38
EPS = 1e-06


def kernel(
    tok_hbm, qkv_ref, ow_ref, conv_hbm, gain_ref, out_ref,
    wkv, wqo, wo, wo_flat, conv_ref, tok_ref, tsib, split, acc, kvt, vals, vin, last_v, last_out, c_all, qb, halo, local,
    part_low, a_in, f_sum, b_in, chip_low, c_in, c_out, readout, mix,
    zkv_r, zqo_r, kvs_r, qos_r, kv_s, qo_s, load_sem,
    tok_sem, kv_sem, o_s, o_r, halo_s, halo_r, a_s, a_r, b_s, b_r, c_s, c_r,
):
    tm = lax.axis_index("tm")
    z = lax.axis_index("space")
    core = lax.rem(tm, 2)
    chip = tm // 2
    x = chip // 4
    y = lax.rem(chip, 4)

    def at(px, py, pc, pz):
        return ((px * 4 + py) * 2 + pc, pz)

    def x_off(i):
        return at(lax.rem(x + i + 4, 4), y, core, z)

    def y_off(i):
        return at(x, lax.rem(y + i + 4, 4), core, z)

    def z_off(i):
        return at(x, y, core, lax.rem(z + i + NZ, NZ))

    sibling = at(x, y, 1 - core, z)

    def remote(src, dst, ssem, rsem, device):
        return pltpu.make_async_remote_copy(
            src_ref=src, dst_ref=dst, send_sem=ssem, recv_sem=rsem,
            device_id=device, device_id_type=MESH,
        )

    slot_tile = [0, 1 + x, 5 + y]
    slot_tile += [1 + lax.rem(x + i, 4) for i in (1, 2, 3)]
    slot_tile += [5 + lax.rem(y + i, 4) for i in (1, 2, 3)]

    def lanes(slot):
        return pl.ds(slot * LANES, LANES)

    def tile_lanes(tile):
        return pl.ds(pl.multiple_of(tile * LANES, LANES), LANES)

    peers = [z_off(1), z_off(-1), z_off(2), z_off(-2), sibling]
    peers += [x_off(i) for i in (1, 2, 3)] + [y_off(i) for i in (1, 2, 3)]
    barrier = pltpu.get_barrier_semaphore()
    for peer in peers:
        pl.semaphore_signal(barrier, inc=1, device_id=peer, device_id_type=MESH)

    def load(slot):
        tile = slot_tile[slot]
        here = wkv.at[z, :, lanes(slot)]
        offset = jnp.where(tile < 4, TILES + 4 * core + tile, 2 * TILES + 4 * core + tile - 4)
        offset = jnp.where(tile == 8, 2 * TILES - 1, offset)
        return pltpu.make_async_copy(qkv_ref.at[:, tile_lanes(offset)], here, load_sem.at[0])

    def load_qo(slot, origin):
        here = wqo.at[z, :, lanes(slot)]
        source = origin.at[:, tile_lanes(slot_tile[slot])]
        return pltpu.make_async_copy(source, here, load_sem.at[1])

    load_tokens = pltpu.make_async_copy(tok_hbm, tok_ref, load_sem.at[2])
    for slot in range(TILES):
        load(slot).start()
    load_tokens.start()
    load_last = pltpu.make_async_copy(
        qkv_ref.at[:, pl.ds((3 * TILES - 1) * LANES, LANES)], last_v, load_sem.at[4]
    )
    load_last.start()

    @pl.when(core == 0)
    def _():
        for slot in range(TILES):
            load_qo(slot, qkv_ref).start()

    @pl.when(core == 1)
    def _():
        for slot in range(TILES):
            load_qo(slot, ow_ref).start()

    load_conv = pltpu.make_async_copy(conv_hbm, conv_ref, load_sem.at[3])
    load_conv.start()

    def local_wait(ref, sem):
        pltpu.make_async_copy(ref, ref, sem).wait()

    local_wait(wkv.at[z], load_sem.at[0])
    load_last.wait()
    my_half = lax.broadcasted_iota(jnp.int32, (1, LANES), 1) // 64 == core
    turn = lax.rem(3 - y + 4, 4)
    last = tile_lanes(jnp.where(turn == 0, 2, 5 + turn))
    rolled = pltpu.roll(last_v[...].astype(jnp.float32), 64, 1)
    merged = jnp.where(my_half, wkv[z, :, last].astype(jnp.float32), rolled)
    wkv[z, :, last] = merged.astype(jnp.bfloat16)
    load_tokens.wait()
    pl.semaphore_wait(barrier, len(peers))

    def step(way, s):
        span = 2 - s % 2
        return z_off(span if way == 0 else -span)

    def z_kv(way, s, t, source):
        ref = wkv.at[source, :, lanes(t)]
        return remote(ref, ref, kv_s.at[0], zkv_r.at[way, s - 1, t], step(way, s))

    def z_qo(way, s, source):
        ref = wqo.at[source, :, pl.ds(0, 3 * LANES)]
        return remote(ref, ref, qo_s.at[0], zqo_r.at[way, s - 1], step(way, s))

    def share(buf, ssem, rsem, source, line, i):
        return remote(
            buf.at[source, :, lanes(1 + line)], buf.at[source, :, lanes(2 + 3 * line + i)],
            ssem, rsem, x_off(-i) if line == 0 else y_off(-i),
        )

    def share_all(buf, ssem, rsem, source):
        for i in (2, 1, 3):
            for line in range(2):
                share(buf, ssem, rsem, source, line, i).start()

    def source_of(way, s):
        return lax.rem(z + NZ - s, NZ) if way == 0 else lax.rem(z + s, NZ)

    for s in (2, 1):
        for t in (1, 2, 0):
            for way in range(2):
                z_kv(way, s, t, z).start()
    token_swap = remote(tok_ref, tsib, tok_sem.at[0], tok_sem.at[1], sibling)
    token_swap.start()
    for block in range(NZ):
        split[block, 0:TOKENS, :] = tok_ref[:, block * ROWS : (block + 1) * ROWS]
    token_swap.wait()
    for block in range(NZ):
        split[block, TOKENS : 2 * TOKENS, :] = tsib[:, block * ROWS : (block + 1) * ROWS]

    def add_source(buf, source, first):
        left = split[source]
        for n in range(3):
            cols = pl.ds(n * 3 * LANES, 3 * LANES)
            term = jnp.dot(left, buf[source, :, cols], preferred_element_type=jnp.float32)
            acc[:, cols] = term if first else acc[:, cols] + term

    add_source(wkv, z, True)

    def pass_kv(m):
        s = 2 * m
        for t in (1, 2, 0):
            for way in range(2):
                @pl.when(s <= 8 - way)
                def _():
                    z_kv(way, s, t, source_of(way, s)).wait_recv()

                @pl.when(s + 2 <= 8 - way)
                def _():
                    z_kv(way, s + 2, t, source_of(way, s)).start()

        for t in (1, 2, 0):
            for way in range(2):
                @pl.when(s + 1 <= 8 - way)
                def _():
                    z_kv(way, s + 1, t, source_of(way, s)).start()

        for odd in range(2):
            for way in range(2):
                @pl.when(s - odd <= 8 - way)
                def _():
                    source = source_of(way, s - odd)
                    if odd:
                        for t in (1, 2, 0):
                            z_kv(way, s - 1, t, source).wait_recv()
                    share_all(wkv, kv_s.at[0], kvs_r.at[way, s - odd - 1], source)

    def take_kv(m):
        for odd in (1, 0):
            s = 2 * m - odd
            for way in range(2):
                @pl.when(s <= 8 - way)
                def _():
                    source = source_of(way, s)
                    shared = wkv.at[source, :, pl.ds(3 * LANES, 6 * LANES)]
                    remote(shared, shared, kv_s.at[0], kvs_r.at[way, s - 1], sibling).wait_recv()
                    add_source(wkv, source, False)

    def start_qo():
        local_wait(wqo.at[z], load_sem.at[1])
        for s in (2, 1):
            for way in range(2):
                z_qo(way, s, z).start()

    def pass_qo(m):
        for odd in range(2):
            s = 2 * m - odd
            for way in range(2):
                @pl.when(s <= 8 - way)
                def _():
                    source = source_of(way, s)
                    z_qo(way, s, source).wait_recv()
                    if odd == 0:
                        for nxt in (2, 1):
                            @pl.when(s + nxt <= 8 - way)
                            def _():
                                z_qo(way, s + nxt, source).start()

                    share_all(wqo, qo_s.at[0], qos_r.at[m - 1], source)

    def o_copy(source, group):
        return remote(wqo.at[source], wo.at[source], o_s.at[0], o_r.at[group], sibling)

    def o_wait(group):
        part = wo.at[0 : (5, 4, 4, 3)[group]]
        remote(part, part, o_s.at[0], o_r.at[group], sibling).wait_recv()

    def sources(m, job):
        def one(k, carry):
            s = 2 * m - k // 2
            source = jnp.where(lax.rem(k, 2) == 0, source_of(0, s), source_of(1, s))

            @pl.when((lax.rem(k, 2) == 0) | (s <= 7))
            def _():
                job(source)

            return carry

        lax.fori_loop(0, 4, one, 0)

    def add_query(buf, source, first):
        left = split[source, 0:TOKENS]
        for n in range(3):
            cols = pl.ds(n * 3 * LANES, 3 * LANES)
            term = jnp.dot(left, buf[source, :, cols], preferred_element_type=jnp.float32)
            acc[0:TOKENS, cols] = term if first else acc[0:TOKENS, cols] + term

    def take_qo(m):
        shared = wqo.at[0 : (3 if m == 4 else 4), :, pl.ds(0, 6 * LANES)]
        remote(shared, shared, qo_s.at[0], qos_r.at[m - 1], sibling).wait_recv()
        if m == 1:
            o_copy(z, 0).start()
        sources(m, lambda source: o_copy(source, m - 1).start())

        def add_all(buf):
            if m == 1:
                add_query(buf, z, True)
            sources(m, lambda source: add_query(buf, source, False))

        @pl.when(core == 0)
        def _():
            add_all(wqo)

        @pl.when(core == 1)
        def _():
            o_wait(m - 1)
            add_all(wo)

    def hook(place):
        for m, passed in ((2, P2), (3, P3), (4, P4)):
            if passed == place:
                pass_qo(m)
        for m, taken in ((1, T1), (2, T2)):
            if taken == place:
                take_qo(m)

    for m in range(1, 6):
        if m <= 4:
            pass_kv(m)
        if m == QO_START:
            start_qo()
        if m == QO_FIRST:
            pass_qo(1)
        if m > 1:
            take_kv(m - 1)
    hook(0)

    for slot in range(TILES):
        tile = slot_tile[slot]
        is_key = (tile < 4) | ((tile == 8) & my_half)
        floor = jnp.where(is_key, 0.0, LOWEST).astype(jnp.float32)
        kvt[:, tile_lanes(tile)] = jnp.maximum(acc[:, lanes(slot)], floor).astype(jnp.bfloat16)

    def last_tile(f):
        both = kvt[f * TOKENS : (f + 1) * TOKENS, lanes(8)].astype(jnp.float32)
        key = jnp.where(my_half, both, 0.0).astype(jnp.bfloat16)
        value = jnp.where(my_half, pltpu.roll(both, 64, 1), 0.0).astype(jnp.bfloat16)
        return key, value

    down = remote(vals.at[pl.ds(3 * COLS, COLS)], halo.at[0], halo_s.at[0], halo_r.at[0], z_off(1))
    up = remote(vals.at[pl.ds(0, COLS)], halo.at[1], halo_s.at[1], halo_r.at[1], z_off(-1))

    row_head = lax.broadcasted_iota(jnp.int32, (LANES, LANES), 0) // 32
    col_head = lax.broadcasted_iota(jnp.int32, (LANES, LANES), 1) // 32
    same_head = row_head == col_head

    mine = jnp.where(z < 8, 8 * core + z, 16 + core)

    def a_copy(d):
        place = z if d < 8 else core * NZ + z
        device = at(x, y, core, d) if d < 8 else at(x, y, d - 8, 8)
        return remote(part_low.at[d], a_in.at[place], a_s.at[0], a_r.at[0], device)

    for j in range(5):
        for f in range(2):
            if j < 4:
                rows = pl.ds(f * TOKENS, TOKENS)
                key, value = kvt[rows, lanes(j)], kvt[rows, lanes(4 + j)]
            else:
                key, value = last_tile(f)
            gram = lax.dot_general(
                key, value, (((0,), (0,)), ((), ())), preferred_element_type=jnp.float32
            )
            gram = jnp.where(same_head, gram, 0.0)
            part = gram[0:32] + gram[32:64] + gram[64:96] + gram[96:128]
            frame = core if f == 0 else 1 - core
            part_low[2 * j, frame] = part[0:16].astype(jnp.bfloat16)
            part_low[2 * j + 1, frame] = part[16:32].astype(jnp.bfloat16)
        for d in (2 * j, 2 * j + 1):
            here = (z == d) if d < 8 else ((z == 8) & (core == d - 8))

            @pl.when(jnp.logical_not(here))
            def _():
                a_copy(d).start()

    last_out[...] = last_tile(1)[1]
    swaps = [
        remote(
            kvt.at[pl.ds(TOKENS, TOKENS), pl.ds(4 * LANES, 4 * LANES)],
            vin.at[:, pl.ds(0, 4 * LANES)], kv_sem.at[0], kv_sem.at[1], sibling,
        ),
        remote(last_out, vin.at[:, lanes(4)], kv_sem.at[2], kv_sem.at[3], sibling),
    ]
    for swap in swaps:
        swap.start()
    hook(5)
    for k in range(4):
        vals[:, tile_lanes(4 * core + k)] = kvt[0:TOKENS, lanes(4 + k)]
    for swap in swaps:
        swap.wait()
    for k in range(4):
        vals[:, tile_lanes(4 * (1 - core) + k)] = vin[:, lanes(k)]
    vals[:, lanes(8)] = last_tile(0)[1] + vin[:, lanes(4)]

    @pl.when(z < NZ - 1)
    def _():
        down.start()

    @pl.when(z > 0)
    def _():
        up.start()

    def local_term():
        @pl.when(z > 0)
        def _():
            down.wait_recv()

        @pl.when(z == 0)
        def _():
            halo[0] = jnp.zeros((COLS, D), jnp.bfloat16)

        @pl.when(z < NZ - 1)
        def _():
            up.wait_recv()

        @pl.when(z == NZ - 1)
        def _():
            halo[1] = jnp.zeros((COLS, D), jnp.bfloat16)

        load_conv.wait()
        col = lax.broadcasted_iota(jnp.int32, (COLS, LANES), 0)

        def conv(j, carry):
            cols = tile_lanes(j)
            weight = [conv_ref[a, :, cols] for a in range(3)]
            sums = [jnp.zeros((COLS, LANES), jnp.float32) for _ in range(4)]
            for row in range(6):
                if row == 0:
                    mid = halo[0, :, cols]
                elif row == 5:
                    mid = halo[1, :, cols]
                else:
                    mid = vals[pl.ds((row - 1) * COLS, COLS), cols]
                mid = mid.astype(jnp.float32)
                left = jnp.where(col == 0, 0.0, pltpu.roll(mid, 1, 0))
                right = jnp.where(col == COLS - 1, 0.0, pltpu.roll(mid, COLS - 1, 0))
                for a in range(3):
                    r = row - a
                    if 0 <= r < 4:
                        sums[r] = (
                            sums[r] + weight[a][0:1] * left + weight[a][1:2] * mid
                            + weight[a][2:3] * right
                        )
            for r in range(4):
                local[pl.ds(r * COLS, COLS), cols] = sums[r]
            return carry

        lax.fori_loop(0, TILES, conv, 0)

    if CONV == 1:
        local_term()
    hook(1)

    hook(2)
    if CONV == 2:
        local_term()

    def b_copy(i):
        later = chip + i
        return remote(chip_low, b_in.at[i - 1], b_s.at[0], b_r.at[0], (later * 2 + core, z))

    def c_copy(pc, k):
        return remote(
            c_out.at[pc], c_in.at[mine], c_s.at[0], c_r.at[0], at(x, y, pc, lax.rem(z + k, NZ))
        )

    far_first = (8, 7, 9, 6, 10, 5, 11, 4, 12, 3, 13, 2, 14, 1, 15)

    @pl.when(z < TILES)
    def _():
        def total(place, own, count):
            a_in[place] = part_low[own]
            others = a_in.at[0 : count - 1]
            remote(others, others, a_s.at[0], a_r.at[0], sibling).wait_recv()
            for frame in range(2):
                f_sum[frame] = jnp.sum(a_in[0:count, frame].astype(jnp.float32), axis=0)

        @pl.when(z < 8)
        def _():
            total(z, z, NZ)

        @pl.when(z == 8)
        def _():
            total(core * NZ + z, 8 + core, 2 * NZ)

        chip_low[...] = (f_sum[0] + f_sum[1]).astype(jnp.bfloat16)
        for i in range(NZ - 1, 0, -1):
            @pl.when(chip + i < NZ)
            def _():
                b_copy(i).start()

    hook(3)
    if CONV == 3:
        local_term()

    @pl.when(z < TILES)
    def _():
        for n in range(1, NZ):
            @pl.when(chip == n)
            def _():
                earlier = b_in.at[0:n]
                remote(earlier, earlier, b_s.at[0], b_r.at[0], sibling).wait_recv()
                f_sum[0] = f_sum[0] + jnp.sum(b_in[0:n].astype(jnp.float32), axis=0)

        c_out[0] = f_sum[0].astype(jnp.bfloat16)
        c_out[1] = (f_sum[0] + f_sum[1]).astype(jnp.bfloat16)
        c_in[mine] = c_out[core]
        for k in far_first:
            for pc in range(2):
                c_copy(pc, k).start()
        for pc in range(2):
            @pl.when(core != pc)
            def _():
                c_copy(pc, 0).start()

    hook(4)
    if CONV == 4:
        local_term()
    take_qo(3)
    take_qo(4)
    for slot in range(TILES):
        qb[:, tile_lanes(slot_tile[slot])] = jnp.maximum(
            acc[0:TOKENS, lanes(slot)], 0.0
        ).astype(jnp.bfloat16)

    def flatten(buf):
        def pair(k, carry):
            for slot in range(TILES):
                both = jnp.concatenate(
                    [
                        buf[2 * k, :, lanes(slot)].astype(jnp.float32),
                        buf[2 * k + 1, :, lanes(slot)].astype(jnp.float32),
                    ],
                    axis=0,
                )
                rows = pl.ds(pl.multiple_of(k * 2 * ROWS, 16), 2 * ROWS)
                wo_flat[rows, lanes(slot)] = both.astype(jnp.bfloat16)
            return carry

        lax.fori_loop(0, NZ // 2, pair, 0)

    @pl.when(core == 0)
    def _():
        for group in range(4):
            o_wait(group)
        flatten(wo)

    @pl.when(core == 1)
    def _():
        flatten(wqo)

    owner = z < TILES

    def wait_c(count):
        rest = c_in.at[0:count]
        remote(rest, rest, c_s.at[0], c_r.at[0], sibling).wait_recv()

    @pl.when(owner)
    def _():
        wait_c(2 * TILES - 1)

    @pl.when(jnp.logical_not(owner))
    def _():
        wait_c(2 * TILES)

    square = jnp.zeros((TOKENS, LANES), jnp.float32)
    for j in range(TILES):
        halves = [c_in[2 * j].astype(jnp.float32), c_in[2 * j + 1].astype(jnp.float32)]
        state = jnp.concatenate(halves * 4, axis=0)
        state = jnp.where(same_head, state, 0.0).astype(jnp.bfloat16)
        term = jnp.dot(qb[:, lanes(j)], state, preferred_element_type=jnp.float32)
        readout[:, lanes(j)] = term
        square = square + term * term
    mean_square = jnp.sum(square, axis=-1, keepdims=True) * (1.0 / D)
    scale = lax.rsqrt(mean_square + EPS)
    for j in range(TILES):
        normed = readout[:, lanes(j)] * scale * gain_ref[lanes(j)].reshape(1, LANES)
        mix[:, lanes(j)] = (normed + local[:, lanes(j)]).astype(jnp.bfloat16)
    for n in range(3):
        cols = pl.ds(n * 3 * LANES, 3 * LANES)
        result = jnp.dot(mix[...], wo_flat[:, cols], preferred_element_type=jnp.float32)
        result = result.astype(jnp.bfloat16)
        for k in range(3):
            out_ref[:, tile_lanes(slot_tile[3 * n + k])] = result[:, k * LANES : (k + 1) * LANES]

    def sent(ref, sem):
        remote(ref, ref, sem, sem, sibling).wait_send()

    sent(wkv.at[0:15], kv_s.at[0])
    sent(wqo.at[0:15], qo_s.at[0])

    @pl.when(owner)
    def _():
        sent(part_low.at[0:9], a_s.at[0])
        sent(c_all.at[0 : 2 * NZ - 1], c_s.at[0])
        for n in range(1, NZ):
            @pl.when(chip + n == NZ - 1)
            def _():
                sent(b_in.at[0:n], b_s.at[0])

    @pl.when(jnp.logical_not(owner))
    def _():
        sent(part_low, a_s.at[0])

    @pl.when(z < NZ - 1)
    def _():
        down.wait_send()

    @pl.when(z > 0)
    def _():
        up.wait_send()

    sent(wqo, o_s.at[0])


def per_device(video_tokens, qkv_weight, out_weight, conv_weight, norm_gain):
    tokens = video_tokens.reshape(TOKENS, D)
    bf16, f32 = jnp.bfloat16, jnp.float32
    vmem = pl.BlockSpec(memory_space=pltpu.VMEM)
    hbm = pl.BlockSpec(memory_space=pltpu.HBM)
    dma = pltpu.SemaphoreType.DMA
    operands = [
        pltpu.with_memory_space_constraint(a, pltpu.HBM)
        for a in (tokens, qkv_weight, out_weight, conv_weight, norm_gain)
    ]
    result = pl.pallas_call(
        kernel,
        out_shape=jax.ShapeDtypeStruct((TOKENS, D), bf16),
        in_specs=[hbm] * 4 + [vmem],
        out_specs=vmem,
        scratch_shapes=[
            pltpu.VMEM((NZ, ROWS, D), bf16),
            pltpu.VMEM((NZ, ROWS, D), bf16),
            pltpu.VMEM((NZ, ROWS, D), bf16),
            pltpu.VMEM((D, D), bf16),
            pltpu.VMEM((3, 3, D), f32),
            pltpu.VMEM((TOKENS, D), bf16),
            pltpu.VMEM((TOKENS, D), bf16),
            pltpu.VMEM((NZ, 2 * TOKENS, ROWS), bf16),
            pltpu.VMEM((2 * TOKENS, D), f32),
            pltpu.VMEM((2 * TOKENS, D), bf16),
            pltpu.VMEM((TOKENS, D), bf16),
            pltpu.VMEM((TOKENS, 5 * LANES), bf16),
            pltpu.VMEM((ROWS, LANES), bf16),
            pltpu.VMEM((TOKENS, LANES), bf16),
            pltpu.VMEM((2 * NZ, 16, LANES), bf16),
            pltpu.VMEM((TOKENS, D), bf16),
            pltpu.VMEM((2, COLS, D), bf16),
            pltpu.VMEM((TOKENS, D), f32),
            pltpu.VMEM((10, 2, 16, LANES), bf16),
            pltpu.VMEM((2 * NZ, 2, 16, LANES), bf16),
            pltpu.VMEM((2, 16, LANES), f32),
            pltpu.VMEM((NZ - 1, 16, LANES), bf16),
            pltpu.VMEM((16, LANES), bf16),
            pltpu.VMEM((2 * TILES, 16, LANES), bf16),
            pltpu.VMEM((2, 16, LANES), bf16),
            pltpu.VMEM((TOKENS, D), f32),
            pltpu.VMEM((TOKENS, D), bf16),
            dma((2, 8, 3)), dma((2, 8)), dma((2, 8)), dma((4,)),
            dma((1,)), dma((1,)), dma((5,)),
            dma((2,)), dma((4,)), dma((1,)), dma((4,)),
            dma((2,)), dma((2,)),
            dma((1,)), dma((1,)), dma((1,)), dma((1,)), dma((1,)), dma((1,)),
        ],
        compiler_params=pltpu.CompilerParams(
            collective_id=0, has_side_effects=True, vmem_limit_bytes=48 * 2**20
        ),
        name="block",
    )(*operands)
    return result.reshape(video_tokens.shape)


def solution(mesh):
    in_specs = (P("tm", "space", None, None), P("space", None), P("space", None), P(), P())
    out_specs = P("tm", "space", None, None)
    return jax.shard_map(
        per_device, mesh=mesh, in_specs=in_specs, out_specs=out_specs, check_vma=False
    )
```

```python
import jax
import jax.numpy as jnp
from jax import lax
from jax.experimental import pallas as pl
from jax.experimental.pallas import tpu as pltpu
from jax.sharding import PartitionSpec as P

MESH = pl.DeviceIdType.MESH
D = 1152
ROWS = 72
TOKENS = 256
COLS = 64
NZ = 16
TILES = 9
LANES = 128
QO_START = 2
QO_FIRST = 4
P2 = 0
P3 = 2
P4 = 3
T1 = 4
CONV = 3
T2 = 4
LOWEST = -3.0e38
EPS = 1e-06


def kernel(
    tok_hbm, qkv_ref, ow_ref, conv_hbm, gain_ref, out_ref,
    wkv, wqo, wo, wo_flat, conv_ref, tok_ref, tsib, split, acc, kvt, vals, vin, last_v, last_out, c_all, qb, halo, local,
    part_low, a_in, f_sum, b_in, chip_low, c_in, c_out, readout, mix,
    zkv_r, zqo_r, kvs_r, qos_r, kv_s, qo_s, load_sem,
    tok_sem, kv_sem, o_s, o_r, halo_s, halo_r, a_s, a_r, b_s, b_r, c_s, c_r,
):
    tm = lax.axis_index("tm")
    z = lax.axis_index("space")
    core = lax.rem(tm, 2)
    chip = tm // 2
    x = chip // 4
    y = lax.rem(chip, 4)

    def at(px, py, pc, pz):
        return ((px * 4 + py) * 2 + pc, pz)

    def x_off(i):
        return at(lax.rem(x + i + 4, 4), y, core, z)

    def y_off(i):
        return at(x, lax.rem(y + i + 4, 4), core, z)

    def z_off(i):
        return at(x, y, core, lax.rem(z + i + NZ, NZ))

    sibling = at(x, y, 1 - core, z)

    def remote(src, dst, ssem, rsem, device):
        return pltpu.make_async_remote_copy(
            src_ref=src, dst_ref=dst, send_sem=ssem, recv_sem=rsem,
            device_id=device, device_id_type=MESH,
        )

    slot_tile = [0, 1 + x, 5 + y]
    slot_tile += [1 + lax.rem(x + i, 4) for i in (1, 2, 3)]
    slot_tile += [5 + lax.rem(y + i, 4) for i in (1, 2, 3)]

    def lanes(slot):
        return pl.ds(slot * LANES, LANES)

    def tile_lanes(tile):
        return pl.ds(pl.multiple_of(tile * LANES, LANES), LANES)

    peers = [z_off(1), z_off(-1), z_off(2), z_off(-2), sibling]
    peers += [x_off(i) for i in (1, 2, 3)] + [y_off(i) for i in (1, 2, 3)]
    barrier = pltpu.get_barrier_semaphore()
    for peer in peers:
        pl.semaphore_signal(barrier, inc=1, device_id=peer, device_id_type=MESH)

    def load(slot):
        tile = slot_tile[slot]
        here = wkv.at[z, :, lanes(slot)]
        offset = jnp.where(tile < 4, TILES + 4 * core + tile, 2 * TILES + 4 * core + tile - 4)
        offset = jnp.where(tile == 8, 2 * TILES - 1, offset)
        return pltpu.make_async_copy(qkv_ref.at[:, tile_lanes(offset)], here, load_sem.at[0])

    def load_qo(slot, origin):
        here = wqo.at[z, :, lanes(slot)]
        source = origin.at[:, tile_lanes(slot_tile[slot])]
        return pltpu.make_async_copy(source, here, load_sem.at[1])

    load_tokens = pltpu.make_async_copy(tok_hbm, tok_ref, load_sem.at[2])
    for slot in range(TILES):
        load(slot).start()
    load_tokens.start()
    load_last = pltpu.make_async_copy(
        qkv_ref.at[:, pl.ds((3 * TILES - 1) * LANES, LANES)], last_v, load_sem.at[4]
    )
    load_last.start()

    @pl.when(core == 0)
    def _():
        for slot in range(TILES):
            load_qo(slot, qkv_ref).start()

    @pl.when(core == 1)
    def _():
        for slot in range(TILES):
            load_qo(slot, ow_ref).start()

    load_conv = pltpu.make_async_copy(conv_hbm, conv_ref, load_sem.at[3])
    load_conv.start()

    def local_wait(ref, sem):
        pltpu.make_async_copy(ref, ref, sem).wait()

    local_wait(wkv.at[z], load_sem.at[0])
    load_last.wait()
    my_half = lax.broadcasted_iota(jnp.int32, (1, LANES), 1) // 64 == core
    turn = lax.rem(3 - y + 4, 4)
    last = tile_lanes(jnp.where(turn == 0, 2, 5 + turn))
    rolled = pltpu.roll(last_v[...].astype(jnp.float32), 64, 1)
    merged = jnp.where(my_half, wkv[z, :, last].astype(jnp.float32), rolled)
    wkv[z, :, last] = merged.astype(jnp.bfloat16)
    load_tokens.wait()
    pl.semaphore_wait(barrier, len(peers))

    def step(way, s):
        span = 2 - s % 2
        return z_off(span if way == 0 else -span)

    def z_kv(way, s, t, source):
        ref = wkv.at[source, :, lanes(t)]
        return remote(ref, ref, kv_s.at[0], zkv_r.at[way, s - 1, t], step(way, s))

    def z_qo(way, s, source):
        ref = wqo.at[source, :, pl.ds(0, 3 * LANES)]
        return remote(ref, ref, qo_s.at[0], zqo_r.at[way, s - 1], step(way, s))

    def share(buf, ssem, rsem, source, line, i):
        return remote(
            buf.at[source, :, lanes(1 + line)], buf.at[source, :, lanes(2 + 3 * line + i)],
            ssem, rsem, x_off(-i) if line == 0 else y_off(-i),
        )

    def share_all(buf, ssem, rsem, source):
        for i in (2, 1, 3):
            for line in range(2):
                share(buf, ssem, rsem, source, line, i).start()

    def source_of(way, s):
        return lax.rem(z + NZ - s, NZ) if way == 0 else lax.rem(z + s, NZ)

    for s in (2, 1):
        for t in (1, 2, 0):
            for way in range(2):
                z_kv(way, s, t, z).start()
    token_swap = remote(tok_ref, tsib, tok_sem.at[0], tok_sem.at[1], sibling)
    token_swap.start()
    for block in range(NZ):
        split[block, 0:TOKENS, :] = tok_ref[:, block * ROWS : (block + 1) * ROWS]
    token_swap.wait()
    for block in range(NZ):
        split[block, TOKENS : 2 * TOKENS, :] = tsib[:, block * ROWS : (block + 1) * ROWS]

    def add_source(buf, source, first):
        left = split[source]
        for n in range(3):
            cols = pl.ds(n * 3 * LANES, 3 * LANES)
            term = jnp.dot(left, buf[source, :, cols], preferred_element_type=jnp.float32)
            acc[:, cols] = term if first else acc[:, cols] + term

    add_source(wkv, z, True)

    def pass_kv(m):
        s = 2 * m
        for t in (1, 2, 0):
            for way in range(2):
                @pl.when(s <= 8 - way)
                def _():
                    z_kv(way, s, t, source_of(way, s)).wait_recv()

                @pl.when(s + 2 <= 8 - way)
                def _():
                    z_kv(way, s + 2, t, source_of(way, s)).start()

        for t in (1, 2, 0):
            for way in range(2):
                @pl.when(s + 1 <= 8 - way)
                def _():
                    z_kv(way, s + 1, t, source_of(way, s)).start()

        for odd in range(2):
            for way in range(2):
                @pl.when(s - odd <= 8 - way)
                def _():
                    source = source_of(way, s - odd)
                    if odd:
                        for t in (1, 2, 0):
                            z_kv(way, s - 1, t, source).wait_recv()
                    share_all(wkv, kv_s.at[0], kvs_r.at[way, s - odd - 1], source)

    def take_kv(m):
        for odd in (1, 0):
            s = 2 * m - odd
            for way in range(2):
                @pl.when(s <= 8 - way)
                def _():
                    source = source_of(way, s)
                    shared = wkv.at[source, :, pl.ds(3 * LANES, 6 * LANES)]
                    remote(shared, shared, kv_s.at[0], kvs_r.at[way, s - 1], sibling).wait_recv()
                    add_source(wkv, source, False)

    def start_qo():
        local_wait(wqo.at[z], load_sem.at[1])
        for s in (2, 1):
            for way in range(2):
                z_qo(way, s, z).start()

    def pass_qo(m):
        for odd in range(2):
            s = 2 * m - odd
            for way in range(2):
                @pl.when(s <= 8 - way)
                def _():
                    source = source_of(way, s)
                    z_qo(way, s, source).wait_recv()
                    if odd == 0:
                        for nxt in (2, 1):
                            @pl.when(s + nxt <= 8 - way)
                            def _():
                                z_qo(way, s + nxt, source).start()

                    share_all(wqo, qo_s.at[0], qos_r.at[m - 1], source)

    def o_copy(source, group):
        return remote(wqo.at[source], wo.at[source], o_s.at[0], o_r.at[group], sibling)

    def o_wait(group):
        part = wo.at[0 : (5, 4, 4, 3)[group]]
        remote(part, part, o_s.at[0], o_r.at[group], sibling).wait_recv()

    def sources(m, job):
        def one(k, carry):
            s = 2 * m - k // 2
            source = jnp.where(lax.rem(k, 2) == 0, source_of(0, s), source_of(1, s))

            @pl.when((lax.rem(k, 2) == 0) | (s <= 7))
            def _():
                job(source)

            return carry

        lax.fori_loop(0, 4, one, 0)

    def add_query(buf, source, first):
        left = split[source, 0:TOKENS]
        for n in range(3):
            cols = pl.ds(n * 3 * LANES, 3 * LANES)
            term = jnp.dot(left, buf[source, :, cols], preferred_element_type=jnp.float32)
            acc[0:TOKENS, cols] = term if first else acc[0:TOKENS, cols] + term

    def take_qo(m):
        shared = wqo.at[0 : (3 if m == 4 else 4), :, pl.ds(0, 6 * LANES)]
        remote(shared, shared, qo_s.at[0], qos_r.at[m - 1], sibling).wait_recv()
        if m == 1:
            o_copy(z, 0).start()
        sources(m, lambda source: o_copy(source, m - 1).start())

        def add_all(buf):
            if m == 1:
                add_query(buf, z, True)
            sources(m, lambda source: add_query(buf, source, False))

        @pl.when(core == 0)
        def _():
            add_all(wqo)

        @pl.when(core == 1)
        def _():
            o_wait(m - 1)
            add_all(wo)

    def hook(place):
        for m, passed in ((2, P2), (3, P3), (4, P4)):
            if passed == place:
                pass_qo(m)
        for m, taken in ((1, T1), (2, T2)):
            if taken == place:
                take_qo(m)

    for m in range(1, 6):
        if m <= 4:
            pass_kv(m)
        if m == QO_START:
            start_qo()
        if m == QO_FIRST:
            pass_qo(1)
        if m > 1:
            take_kv(m - 1)
    hook(0)

    for slot in range(TILES):
        tile = slot_tile[slot]
        is_key = (tile < 4) | ((tile == 8) & my_half)
        floor = jnp.where(is_key, 0.0, LOWEST).astype(jnp.float32)
        kvt[:, tile_lanes(tile)] = jnp.maximum(acc[:, lanes(slot)], floor).astype(jnp.bfloat16)

    def last_tile(f):
        both = kvt[f * TOKENS : (f + 1) * TOKENS, lanes(8)].astype(jnp.float32)
        key = jnp.where(my_half, both, 0.0).astype(jnp.bfloat16)
        value = jnp.where(my_half, pltpu.roll(both, 64, 1), 0.0).astype(jnp.bfloat16)
        return key, value

    down = remote(vals.at[pl.ds(3 * COLS, COLS)], halo.at[0], halo_s.at[0], halo_r.at[0], z_off(1))
    up = remote(vals.at[pl.ds(0, COLS)], halo.at[1], halo_s.at[1], halo_r.at[1], z_off(-1))

    row_head = lax.broadcasted_iota(jnp.int32, (LANES, LANES), 0) // 32
    col_head = lax.broadcasted_iota(jnp.int32, (LANES, LANES), 1) // 32
    same_head = row_head == col_head

    mine = jnp.where(z < 8, 8 * core + z, 16 + core)

    def a_copy(d):
        place = z if d < 8 else core * NZ + z
        device = at(x, y, core, d) if d < 8 else at(x, y, d - 8, 8)
        return remote(part_low.at[d], a_in.at[place], a_s.at[0], a_r.at[0], device)

    for j in range(5):
        for f in range(2):
            if j < 4:
                rows = pl.ds(f * TOKENS, TOKENS)
                key, value = kvt[rows, lanes(j)], kvt[rows, lanes(4 + j)]
            else:
                key, value = last_tile(f)
            gram = lax.dot_general(
                key, value, (((0,), (0,)), ((), ())), preferred_element_type=jnp.float32
            )
            gram = jnp.where(same_head, gram, 0.0)
            part = gram[0:32] + gram[32:64] + gram[64:96] + gram[96:128]
            frame = core if f == 0 else 1 - core
            part_low[2 * j, frame] = part[0:16].astype(jnp.bfloat16)
            part_low[2 * j + 1, frame] = part[16:32].astype(jnp.bfloat16)
        for d in (2 * j, 2 * j + 1):
            here = (z == d) if d < 8 else ((z == 8) & (core == d - 8))

            @pl.when(jnp.logical_not(here))
            def _():
                a_copy(d).start()

    last_out[...] = last_tile(1)[1]
    swaps = [
        remote(
            kvt.at[pl.ds(TOKENS, TOKENS), pl.ds(4 * LANES, 4 * LANES)],
            vin.at[:, pl.ds(0, 4 * LANES)], kv_sem.at[0], kv_sem.at[1], sibling,
        ),
        remote(last_out, vin.at[:, lanes(4)], kv_sem.at[2], kv_sem.at[3], sibling),
    ]
    for swap in swaps:
        swap.start()
    hook(5)
    for k in range(4):
        vals[:, tile_lanes(4 * core + k)] = kvt[0:TOKENS, lanes(4 + k)]
    for swap in swaps:
        swap.wait()
    for k in range(4):
        vals[:, tile_lanes(4 * (1 - core) + k)] = vin[:, lanes(k)]
    vals[:, lanes(8)] = last_tile(0)[1] + vin[:, lanes(4)]

    @pl.when(z < NZ - 1)
    def _():
        down.start()

    @pl.when(z > 0)
    def _():
        up.start()

    def local_term():
        @pl.when(z > 0)
        def _():
            down.wait_recv()

        @pl.when(z == 0)
        def _():
            halo[0] = jnp.zeros((COLS, D), jnp.bfloat16)

        @pl.when(z < NZ - 1)
        def _():
            up.wait_recv()

        @pl.when(z == NZ - 1)
        def _():
            halo[1] = jnp.zeros((COLS, D), jnp.bfloat16)

        load_conv.wait()
        col = lax.broadcasted_iota(jnp.int32, (COLS, LANES), 0)

        def conv(j, carry):
            cols = tile_lanes(j)
            weight = [conv_ref[a, :, cols] for a in range(3)]
            sums = [jnp.zeros((COLS, LANES), jnp.float32) for _ in range(4)]
            for row in range(6):
                if row == 0:
                    mid = halo[0, :, cols]
                elif row == 5:
                    mid = halo[1, :, cols]
                else:
                    mid = vals[pl.ds((row - 1) * COLS, COLS), cols]
                mid = mid.astype(jnp.float32)
                left = jnp.where(col == 0, 0.0, pltpu.roll(mid, 1, 0))
                right = jnp.where(col == COLS - 1, 0.0, pltpu.roll(mid, COLS - 1, 0))
                for a in range(3):
                    r = row - a
                    if 0 <= r < 4:
                        sums[r] = (
                            sums[r] + weight[a][0:1] * left + weight[a][1:2] * mid
                            + weight[a][2:3] * right
                        )
            for r in range(4):
                local[pl.ds(r * COLS, COLS), cols] = sums[r]
            return carry

        lax.fori_loop(0, TILES, conv, 0)

    if CONV == 1:
        local_term()
    hook(1)

    hook(2)
    if CONV == 2:
        local_term()

    def b_copy(i):
        later = chip + i
        return remote(chip_low, b_in.at[i - 1], b_s.at[0], b_r.at[0], (later * 2 + core, z))

    def c_copy(pc, k):
        return remote(
            c_out.at[pc], c_in.at[mine], c_s.at[0], c_r.at[0], at(x, y, pc, lax.rem(z + k, NZ))
        )

    far_first = (8, 7, 9, 6, 10, 5, 11, 4, 12, 3, 13, 2, 14, 1, 15)

    @pl.when(z < TILES)
    def _():
        def total(place, own, count):
            a_in[place] = part_low[own]
            others = a_in.at[0 : count - 1]
            remote(others, others, a_s.at[0], a_r.at[0], sibling).wait_recv()
            for frame in range(2):
                f_sum[frame] = jnp.sum(a_in[0:count, frame].astype(jnp.float32), axis=0)

        @pl.when(z < 8)
        def _():
            total(z, z, NZ)

        @pl.when(z == 8)
        def _():
            total(core * NZ + z, 8 + core, 2 * NZ)

        chip_low[...] = (f_sum[0] + f_sum[1]).astype(jnp.bfloat16)
        for i in range(NZ - 1, 0, -1):
            @pl.when(chip + i < NZ)
            def _():
                b_copy(i).start()

    hook(3)
    if CONV == 3:
        local_term()

    @pl.when(z < TILES)
    def _():
        for n in range(1, NZ):
            @pl.when(chip == n)
            def _():
                earlier = b_in.at[0:n]
                remote(earlier, earlier, b_s.at[0], b_r.at[0], sibling).wait_recv()
                f_sum[0] = f_sum[0] + jnp.sum(b_in[0:n].astype(jnp.float32), axis=0)

        c_out[0] = f_sum[0].astype(jnp.bfloat16)
        c_out[1] = (f_sum[0] + f_sum[1]).astype(jnp.bfloat16)
        c_in[mine] = c_out[core]
        for k in far_first:
            for pc in range(2):
                c_copy(pc, k).start()
        for pc in range(2):
            @pl.when(core != pc)
            def _():
                c_copy(pc, 0).start()

    hook(4)
    if CONV == 4:
        local_term()
    take_qo(3)
    take_qo(4)
    for slot in range(TILES):
        qb[:, tile_lanes(slot_tile[slot])] = jnp.maximum(
            acc[0:TOKENS, lanes(slot)], 0.0
        ).astype(jnp.bfloat16)

    def flatten(buf):
        def pair(k, carry):
            for slot in range(TILES):
                both = jnp.concatenate(
                    [
                        buf[2 * k, :, lanes(slot)].astype(jnp.float32),
                        buf[2 * k + 1, :, lanes(slot)].astype(jnp.float32),
                    ],
                    axis=0,
                )
                rows = pl.ds(pl.multiple_of(k * 2 * ROWS, 16), 2 * ROWS)
                wo_flat[rows, lanes(slot)] = both.astype(jnp.bfloat16)
            return carry

        lax.fori_loop(0, NZ // 2, pair, 0)

    @pl.when(core == 0)
    def _():
        for group in range(4):
            o_wait(group)
        flatten(wo)

    @pl.when(core == 1)
    def _():
        flatten(wqo)

    owner = z < TILES

    def wait_c(count):
        rest = c_in.at[0:count]
        remote(rest, rest, c_s.at[0], c_r.at[0], sibling).wait_recv()

    @pl.when(owner)
    def _():
        wait_c(2 * TILES - 1)

    @pl.when(jnp.logical_not(owner))
    def _():
        wait_c(2 * TILES)

    square = jnp.zeros((TOKENS, LANES), jnp.float32)
    for j in range(TILES):
        halves = [c_in[2 * j].astype(jnp.float32), c_in[2 * j + 1].astype(jnp.float32)]
        state = jnp.concatenate(halves * 4, axis=0)
        state = jnp.where(same_head, state, 0.0).astype(jnp.bfloat16)
        term = jnp.dot(qb[:, lanes(j)], state, preferred_element_type=jnp.float32)
        readout[:, lanes(j)] = term
        square = square + term * term
    mean_square = jnp.sum(square, axis=-1, keepdims=True) * (1.0 / D)
    scale = lax.rsqrt(mean_square + EPS)
    for j in range(TILES):
        normed = readout[:, lanes(j)] * scale * gain_ref[lanes(j)].reshape(1, LANES)
        mix[:, lanes(j)] = (normed + local[:, lanes(j)]).astype(jnp.bfloat16)
    for n in range(3):
        cols = pl.ds(n * 3 * LANES, 3 * LANES)
        result = jnp.dot(mix[...], wo_flat[:, cols], preferred_element_type=jnp.float32)
        result = result.astype(jnp.bfloat16)
        for k in range(3):
            out_ref[:, tile_lanes(slot_tile[3 * n + k])] = result[:, k * LANES : (k + 1) * LANES]

    def sent(ref, sem):
        remote(ref, ref, sem, sem, sibling).wait_send()

    sent(wkv.at[0:15], kv_s.at[0])
    sent(wqo.at[0:15], qo_s.at[0])

    @pl.when(owner)
    def _():
        sent(part_low.at[0:9], a_s.at[0])
        sent(c_all.at[0 : 2 * NZ - 1], c_s.at[0])
        for n in range(1, NZ):
            @pl.when(chip + n == NZ - 1)
            def _():
                sent(b_in.at[0:n], b_s.at[0])

    @pl.when(jnp.logical_not(owner))
    def _():
        sent(part_low, a_s.at[0])

    @pl.when(z < NZ - 1)
    def _():
        down.wait_send()

    @pl.when(z > 0)
    def _():
        up.wait_send()

    sent(wqo, o_s.at[0])


def per_device(video_tokens, qkv_weight, out_weight, conv_weight, norm_gain):
    tokens = video_tokens.reshape(TOKENS, D)
    bf16, f32 = jnp.bfloat16, jnp.float32
    vmem = pl.BlockSpec(memory_space=pltpu.VMEM)
    hbm = pl.BlockSpec(memory_space=pltpu.HBM)
    dma = pltpu.SemaphoreType.DMA
    operands = [
        pltpu.with_memory_space_constraint(a, pltpu.HBM)
        for a in (tokens, qkv_weight, out_weight, conv_weight, norm_gain)
    ]
    result = pl.pallas_call(
        kernel,
        out_shape=jax.ShapeDtypeStruct((TOKENS, D), bf16),
        in_specs=[hbm] * 4 + [vmem],
        out_specs=vmem,
        scratch_shapes=[
            pltpu.VMEM((NZ, ROWS, D), bf16),
            pltpu.VMEM((NZ, ROWS, D), bf16),
            pltpu.VMEM((NZ, ROWS, D), bf16),
            pltpu.VMEM((D, D), bf16),
            pltpu.VMEM((3, 3, D), f32),
            pltpu.VMEM((TOKENS, D), bf16),
            pltpu.VMEM((TOKENS, D), bf16),
            pltpu.VMEM((NZ, 2 * TOKENS, ROWS), bf16),
            pltpu.VMEM((2 * TOKENS, D), f32),
            pltpu.VMEM((2 * TOKENS, D), bf16),
            pltpu.VMEM((TOKENS, D), bf16),
            pltpu.VMEM((TOKENS, 5 * LANES), bf16),
            pltpu.VMEM((ROWS, LANES), bf16),
            pltpu.VMEM((TOKENS, LANES), bf16),
            pltpu.VMEM((2 * NZ, 16, LANES), bf16),
            pltpu.VMEM((TOKENS, D), bf16),
            pltpu.VMEM((2, COLS, D), bf16),
            pltpu.VMEM((TOKENS, D), f32),
            pltpu.VMEM((10, 2, 16, LANES), bf16),
            pltpu.VMEM((2 * NZ, 2, 16, LANES), bf16),
            pltpu.VMEM((2, 16, LANES), f32),
            pltpu.VMEM((NZ - 1, 16, LANES), bf16),
            pltpu.VMEM((16, LANES), bf16),
            pltpu.VMEM((2 * TILES, 16, LANES), bf16),
            pltpu.VMEM((2, 16, LANES), bf16),
            pltpu.VMEM((TOKENS, D), f32),
            pltpu.VMEM((TOKENS, D), bf16),
            dma((2, 8, 3)), dma((2, 8)), dma((2, 8)), dma((4,)),
            dma((1,)), dma((1,)), dma((5,)),
            dma((2,)), dma((4,)), dma((1,)), dma((4,)),
            dma((2,)), dma((2,)),
            dma((1,)), dma((1,)), dma((1,)), dma((1,)), dma((1,)), dma((1,)),
        ],
        compiler_params=pltpu.CompilerParams(
            collective_id=0, has_side_effects=True, vmem_limit_bytes=48 * 2**20
        ),
        name="block",
    )(*operands)
    return result.reshape(video_tokens.shape)


def solution(mesh):
    in_specs = (P("tm", "space", None, None), P("space", None), P("space", None), P(), P())
    out_specs = P("tm", "space", None, None)
    return jax.shard_map(
        per_device, mesh=mesh, in_specs=in_specs, out_specs=out_specs, check_vma=False
    )
```

```python
import jax
import jax.numpy as jnp
from jax import lax
from jax.experimental import pallas as pl
from jax.experimental.pallas import tpu as pltpu
from jax.sharding import PartitionSpec as P

MESH = pl.DeviceIdType.MESH
D = 1152
ROWS = 72
TOKENS = 256
COLS = 64
NZ = 16
TILES = 9
LANES = 128
QO_START = 2
QO_FIRST = 4
P2 = 0
P3 = 2
P4 = 3
T1 = 4
CONV = 3
T2 = 4
LOWEST = -3.0e38
EPS = 1e-06


def kernel(
    tok_hbm, qkv_ref, ow_ref, conv_hbm, gain_ref, out_ref,
    wkv, wqo, wo, wo_flat, conv_ref, tok_ref, tsib, split, acc, kvt, vals, vin, last_v, last_out, c_all, qb, halo, local,
    part_low, a_in, f_sum, b_in, chip_low, c_in, c_out, readout, mix,
    zkv_r, zqo_r, kvs_r, qos_r, kv_s, qo_s, load_sem,
    tok_sem, kv_sem, o_s, o_r, halo_s, halo_r, a_s, a_r, b_s, b_r, c_s, c_r,
):
    tm = lax.axis_index("tm")
    z = lax.axis_index("space")
    core = lax.rem(tm, 2)
    chip = tm // 2
    x = chip // 4
    y = lax.rem(chip, 4)

    def at(px, py, pc, pz):
        return ((px * 4 + py) * 2 + pc, pz)

    def x_off(i):
        return at(lax.rem(x + i + 4, 4), y, core, z)

    def y_off(i):
        return at(x, lax.rem(y + i + 4, 4), core, z)

    def z_off(i):
        return at(x, y, core, lax.rem(z + i + NZ, NZ))

    sibling = at(x, y, 1 - core, z)

    def remote(src, dst, ssem, rsem, device):
        return pltpu.make_async_remote_copy(
            src_ref=src, dst_ref=dst, send_sem=ssem, recv_sem=rsem,
            device_id=device, device_id_type=MESH,
        )

    slot_tile = [0, 1 + x, 5 + y]
    slot_tile += [1 + lax.rem(x + i, 4) for i in (1, 2, 3)]
    slot_tile += [5 + lax.rem(y + i, 4) for i in (1, 2, 3)]

    def lanes(slot):
        return pl.ds(slot * LANES, LANES)

    def tile_lanes(tile):
        return pl.ds(pl.multiple_of(tile * LANES, LANES), LANES)

    peers = [z_off(1), z_off(-1), z_off(2), z_off(-2), sibling]
    peers += [x_off(i) for i in (1, 2, 3)] + [y_off(i) for i in (1, 2, 3)]
    barrier = pltpu.get_barrier_semaphore()
    for peer in peers:
        pl.semaphore_signal(barrier, inc=1, device_id=peer, device_id_type=MESH)

    def load(slot):
        tile = slot_tile[slot]
        here = wkv.at[z, :, lanes(slot)]
        offset = jnp.where(tile < 4, TILES + 4 * core + tile, 2 * TILES + 4 * core + tile - 4)
        offset = jnp.where(tile == 8, 2 * TILES - 1, offset)
        return pltpu.make_async_copy(qkv_ref.at[:, tile_lanes(offset)], here, load_sem.at[0])

    def load_qo(slot, origin):
        here = wqo.at[z, :, lanes(slot)]
        source = origin.at[:, tile_lanes(slot_tile[slot])]
        return pltpu.make_async_copy(source, here, load_sem.at[1])

    load_tokens = pltpu.make_async_copy(tok_hbm, tok_ref, load_sem.at[2])
    for slot in range(TILES):
        load(slot).start()
    load_tokens.start()
    load_last = pltpu.make_async_copy(
        qkv_ref.at[:, pl.ds((3 * TILES - 1) * LANES, LANES)], last_v, load_sem.at[4]
    )
    load_last.start()

    @pl.when(core == 0)
    def _():
        for slot in range(TILES):
            load_qo(slot, qkv_ref).start()

    @pl.when(core == 1)
    def _():
        for slot in range(TILES):
            load_qo(slot, ow_ref).start()

    load_conv = pltpu.make_async_copy(conv_hbm, conv_ref, load_sem.at[3])
    load_conv.start()

    def local_wait(ref, sem):
        pltpu.make_async_copy(ref, ref, sem).wait()

    local_wait(wkv.at[z], load_sem.at[0])
    load_last.wait()
    my_half = lax.broadcasted_iota(jnp.int32, (1, LANES), 1) // 64 == core
    turn = lax.rem(3 - y + 4, 4)
    last = tile_lanes(jnp.where(turn == 0, 2, 5 + turn))
    rolled = pltpu.roll(last_v[...].astype(jnp.float32), 64, 1)
    merged = jnp.where(my_half, wkv[z, :, last].astype(jnp.float32), rolled)
    wkv[z, :, last] = merged.astype(jnp.bfloat16)
    load_tokens.wait()
    pl.semaphore_wait(barrier, len(peers))

    def step(way, s):
        span = 2 - s % 2
        return z_off(span if way == 0 else -span)

    def z_kv(way, s, t, source):
        ref = wkv.at[source, :, lanes(t)]
        return remote(ref, ref, kv_s.at[0], zkv_r.at[way, s - 1, t], step(way, s))

    def z_qo(way, s, source):
        ref = wqo.at[source, :, pl.ds(0, 3 * LANES)]
        return remote(ref, ref, qo_s.at[0], zqo_r.at[way, s - 1], step(way, s))

    def share(buf, ssem, rsem, source, line, i):
        return remote(
            buf.at[source, :, lanes(1 + line)], buf.at[source, :, lanes(2 + 3 * line + i)],
            ssem, rsem, x_off(-i) if line == 0 else y_off(-i),
        )

    def share_all(buf, ssem, rsem, source):
        for i in (2, 1, 3):
            for line in range(2):
                share(buf, ssem, rsem, source, line, i).start()

    def source_of(way, s):
        return lax.rem(z + NZ - s, NZ) if way == 0 else lax.rem(z + s, NZ)

    for s in (2, 1):
        for t in (1, 2, 0):
            for way in range(2):
                z_kv(way, s, t, z).start()
    token_swap = remote(tok_ref, tsib, tok_sem.at[0], tok_sem.at[1], sibling)
    token_swap.start()
    for block in range(NZ):
        split[block, 0:TOKENS, :] = tok_ref[:, block * ROWS : (block + 1) * ROWS]
    token_swap.wait()
    for block in range(NZ):
        split[block, TOKENS : 2 * TOKENS, :] = tsib[:, block * ROWS : (block + 1) * ROWS]

    def add_source(buf, source, first):
        left = split[source]
        for n in range(3):
            cols = pl.ds(n * 3 * LANES, 3 * LANES)
            term = jnp.dot(left, buf[source, :, cols], preferred_element_type=jnp.float32)
            acc[:, cols] = term if first else acc[:, cols] + term

    add_source(wkv, z, True)

    def pass_kv(m):
        s = 2 * m
        for t in (1, 2, 0):
            for way in range(2):
                @pl.when(s <= 8 - way)
                def _():
                    z_kv(way, s, t, source_of(way, s)).wait_recv()

                @pl.when(s + 2 <= 8 - way)
                def _():
                    z_kv(way, s + 2, t, source_of(way, s)).start()

        for t in (1, 2, 0):
            for way in range(2):
                @pl.when(s + 1 <= 8 - way)
                def _():
                    z_kv(way, s + 1, t, source_of(way, s)).start()

        for odd in range(2):
            for way in range(2):
                @pl.when(s - odd <= 8 - way)
                def _():
                    source = source_of(way, s - odd)
                    if odd:
                        for t in (1, 2, 0):
                            z_kv(way, s - 1, t, source).wait_recv()
                    share_all(wkv, kv_s.at[0], kvs_r.at[way, s - odd - 1], source)

    def take_kv(m):
        for odd in (0, 1):
            s = 2 * m - odd
            for way in range(2):
                @pl.when(s <= 8 - way)
                def _():
                    source = source_of(way, s)
                    shared = wkv.at[source, :, pl.ds(3 * LANES, 6 * LANES)]
                    remote(shared, shared, kv_s.at[0], kvs_r.at[way, s - 1], sibling).wait_recv()
                    add_source(wkv, source, False)

    def start_qo():
        local_wait(wqo.at[z], load_sem.at[1])
        for s in (2, 1):
            for way in range(2):
                z_qo(way, s, z).start()

    def pass_qo(m):
        for odd in range(2):
            s = 2 * m - odd
            for way in range(2):
                @pl.when(s <= 8 - way)
                def _():
                    source = source_of(way, s)
                    z_qo(way, s, source).wait_recv()
                    if odd == 0:
                        for nxt in (2, 1):
                            @pl.when(s + nxt <= 8 - way)
                            def _():
                                z_qo(way, s + nxt, source).start()

                    share_all(wqo, qo_s.at[0], qos_r.at[m - 1], source)

    def o_copy(source, group):
        return remote(wqo.at[source], wo.at[source], o_s.at[0], o_r.at[group], sibling)

    def o_wait(group):
        part = wo.at[0 : (5, 4, 4, 3)[group]]
        remote(part, part, o_s.at[0], o_r.at[group], sibling).wait_recv()

    def sources(m, job):
        def one(k, carry):
            s = 2 * m - k // 2
            source = jnp.where(lax.rem(k, 2) == 0, source_of(0, s), source_of(1, s))

            @pl.when((lax.rem(k, 2) == 0) | (s <= 7))
            def _():
                job(source)

            return carry

        lax.fori_loop(0, 4, one, 0)

    def add_query(buf, source, first):
        left = split[source, 0:TOKENS]
        for n in range(3):
            cols = pl.ds(n * 3 * LANES, 3 * LANES)
            term = jnp.dot(left, buf[source, :, cols], preferred_element_type=jnp.float32)
            acc[0:TOKENS, cols] = term if first else acc[0:TOKENS, cols] + term

    def take_qo(m):
        shared = wqo.at[0 : (3 if m == 4 else 4), :, pl.ds(0, 6 * LANES)]
        remote(shared, shared, qo_s.at[0], qos_r.at[m - 1], sibling).wait_recv()
        if m == 1:
            o_copy(z, 0).start()
        sources(m, lambda source: o_copy(source, m - 1).start())

        def add_all(buf):
            if m == 1:
                add_query(buf, z, True)
            sources(m, lambda source: add_query(buf, source, False))

        @pl.when(core == 0)
        def _():
            add_all(wqo)

        @pl.when(core == 1)
        def _():
            o_wait(m - 1)
            add_all(wo)

    def hook(place):
        for m, passed in ((2, P2), (3, P3), (4, P4)):
            if passed == place:
                pass_qo(m)
        for m, taken in ((1, T1), (2, T2)):
            if taken == place:
                take_qo(m)

    for m in range(1, 6):
        if m <= 4:
            pass_kv(m)
        if m == QO_START:
            start_qo()
        if m == QO_FIRST:
            pass_qo(1)
        if m > 1:
            take_kv(m - 1)
    hook(0)

    for slot in range(TILES):
        tile = slot_tile[slot]
        is_key = (tile < 4) | ((tile == 8) & my_half)
        floor = jnp.where(is_key, 0.0, LOWEST).astype(jnp.float32)
        kvt[:, tile_lanes(tile)] = jnp.maximum(acc[:, lanes(slot)], floor).astype(jnp.bfloat16)

    def last_tile(f):
        both = kvt[f * TOKENS : (f + 1) * TOKENS, lanes(8)].astype(jnp.float32)
        key = jnp.where(my_half, both, 0.0).astype(jnp.bfloat16)
        value = jnp.where(my_half, pltpu.roll(both, 64, 1), 0.0).astype(jnp.bfloat16)
        return key, value

    down = remote(vals.at[pl.ds(3 * COLS, COLS)], halo.at[0], halo_s.at[0], halo_r.at[0], z_off(1))
    up = remote(vals.at[pl.ds(0, COLS)], halo.at[1], halo_s.at[1], halo_r.at[1], z_off(-1))

    row_head = lax.broadcasted_iota(jnp.int32, (LANES, LANES), 0) // 32
    col_head = lax.broadcasted_iota(jnp.int32, (LANES, LANES), 1) // 32
    same_head = row_head == col_head

    mine = jnp.where(z < 8, 8 * core + z, 16 + core)

    def a_copy(d):
        place = z if d < 8 else core * NZ + z
        device = at(x, y, core, d) if d < 8 else at(x, y, d - 8, 8)
        return remote(part_low.at[d], a_in.at[place], a_s.at[0], a_r.at[0], device)

    for j in range(5):
        for f in range(2):
            if j < 4:
                rows = pl.ds(f * TOKENS, TOKENS)
                key, value = kvt[rows, lanes(j)], kvt[rows, lanes(4 + j)]
            else:
                key, value = last_tile(f)
            gram = lax.dot_general(
                key, value, (((0,), (0,)), ((), ())), preferred_element_type=jnp.float32
            )
            gram = jnp.where(same_head, gram, 0.0)
            part = gram[0:32] + gram[32:64] + gram[64:96] + gram[96:128]
            frame = core if f == 0 else 1 - core
            part_low[2 * j, frame] = part[0:16].astype(jnp.bfloat16)
            part_low[2 * j + 1, frame] = part[16:32].astype(jnp.bfloat16)
        for d in (2 * j, 2 * j + 1):
            here = (z == d) if d < 8 else ((z == 8) & (core == d - 8))

            @pl.when(jnp.logical_not(here))
            def _():
                a_copy(d).start()

    last_out[...] = last_tile(1)[1]
    swaps = [
        remote(
            kvt.at[pl.ds(TOKENS, TOKENS), pl.ds(4 * LANES, 4 * LANES)],
            vin.at[:, pl.ds(0, 4 * LANES)], kv_sem.at[0], kv_sem.at[1], sibling,
        ),
        remote(last_out, vin.at[:, lanes(4)], kv_sem.at[2], kv_sem.at[3], sibling),
    ]
    for swap in swaps:
        swap.start()
    hook(5)
    for k in range(4):
        vals[:, tile_lanes(4 * core + k)] = kvt[0:TOKENS, lanes(4 + k)]
    for swap in swaps:
        swap.wait()
    for k in range(4):
        vals[:, tile_lanes(4 * (1 - core) + k)] = vin[:, lanes(k)]
    vals[:, lanes(8)] = last_tile(0)[1] + vin[:, lanes(4)]

    @pl.when(z < NZ - 1)
    def _():
        down.start()

    @pl.when(z > 0)
    def _():
        up.start()

    def local_term():
        @pl.when(z > 0)
        def _():
            down.wait_recv()

        @pl.when(z == 0)
        def _():
            halo[0] = jnp.zeros((COLS, D), jnp.bfloat16)

        @pl.when(z < NZ - 1)
        def _():
            up.wait_recv()

        @pl.when(z == NZ - 1)
        def _():
            halo[1] = jnp.zeros((COLS, D), jnp.bfloat16)

        load_conv.wait()
        col = lax.broadcasted_iota(jnp.int32, (COLS, LANES), 0)

        def conv(j, carry):
            cols = tile_lanes(j)
            weight = [conv_ref[a, :, cols] for a in range(3)]
            sums = [jnp.zeros((COLS, LANES), jnp.float32) for _ in range(4)]
            for row in range(6):
                if row == 0:
                    mid = halo[0, :, cols]
                elif row == 5:
                    mid = halo[1, :, cols]
                else:
                    mid = vals[pl.ds((row - 1) * COLS, COLS), cols]
                mid = mid.astype(jnp.float32)
                left = jnp.where(col == 0, 0.0, pltpu.roll(mid, 1, 0))
                right = jnp.where(col == COLS - 1, 0.0, pltpu.roll(mid, COLS - 1, 0))
                for a in range(3):
                    r = row - a
                    if 0 <= r < 4:
                        sums[r] = (
                            sums[r] + weight[a][0:1] * left + weight[a][1:2] * mid
                            + weight[a][2:3] * right
                        )
            for r in range(4):
                local[pl.ds(r * COLS, COLS), cols] = sums[r]
            return carry

        lax.fori_loop(0, TILES, conv, 0)

    if CONV == 1:
        local_term()
    hook(1)

    hook(2)
    if CONV == 2:
        local_term()

    def b_copy(i):
        later = chip + i
        return remote(chip_low, b_in.at[i - 1], b_s.at[0], b_r.at[0], (later * 2 + core, z))

    def c_copy(pc, k):
        return remote(
            c_out.at[pc], c_in.at[mine], c_s.at[0], c_r.at[0], at(x, y, pc, lax.rem(z + k, NZ))
        )

    far_first = (8, 7, 9, 6, 10, 5, 11, 4, 12, 3, 13, 2, 14, 1, 15)

    @pl.when(z < TILES)
    def _():
        def total(place, own, count):
            a_in[place] = part_low[own]
            others = a_in.at[0 : count - 1]
            remote(others, others, a_s.at[0], a_r.at[0], sibling).wait_recv()
            for frame in range(2):
                f_sum[frame] = jnp.sum(a_in[0:count, frame].astype(jnp.float32), axis=0)

        @pl.when(z < 8)
        def _():
            total(z, z, NZ)

        @pl.when(z == 8)
        def _():
            total(core * NZ + z, 8 + core, 2 * NZ)

        chip_low[...] = (f_sum[0] + f_sum[1]).astype(jnp.bfloat16)
        for i in range(NZ - 1, 0, -1):
            @pl.when(chip + i < NZ)
            def _():
                b_copy(i).start()

    hook(3)
    if CONV == 3:
        local_term()

    @pl.when(z < TILES)
    def _():
        for n in range(1, NZ):
            @pl.when(chip == n)
            def _():
                earlier = b_in.at[0:n]
                remote(earlier, earlier, b_s.at[0], b_r.at[0], sibling).wait_recv()
                f_sum[0] = f_sum[0] + jnp.sum(b_in[0:n].astype(jnp.float32), axis=0)

        c_out[0] = f_sum[0].astype(jnp.bfloat16)
        c_out[1] = (f_sum[0] + f_sum[1]).astype(jnp.bfloat16)
        c_in[mine] = c_out[core]
        for k in far_first:
            for pc in range(2):
                c_copy(pc, k).start()
        for pc in range(2):
            @pl.when(core != pc)
            def _():
                c_copy(pc, 0).start()

    hook(4)
    if CONV == 4:
        local_term()
    take_qo(3)
    take_qo(4)
    for slot in range(TILES):
        qb[:, tile_lanes(slot_tile[slot])] = jnp.maximum(
            acc[0:TOKENS, lanes(slot)], 0.0
        ).astype(jnp.bfloat16)

    def flatten(buf):
        def pair(k, carry):
            for slot in range(TILES):
                both = jnp.concatenate(
                    [
                        buf[2 * k, :, lanes(slot)].astype(jnp.float32),
                        buf[2 * k + 1, :, lanes(slot)].astype(jnp.float32),
                    ],
                    axis=0,
                )
                rows = pl.ds(pl.multiple_of(k * 2 * ROWS, 16), 2 * ROWS)
                wo_flat[rows, lanes(slot)] = both.astype(jnp.bfloat16)
            return carry

        lax.fori_loop(0, NZ // 2, pair, 0)

    @pl.when(core == 0)
    def _():
        for group in range(4):
            o_wait(group)
        flatten(wo)

    @pl.when(core == 1)
    def _():
        flatten(wqo)

    owner = z < TILES

    def wait_c(count):
        rest = c_in.at[0:count]
        remote(rest, rest, c_s.at[0], c_r.at[0], sibling).wait_recv()

    @pl.when(owner)
    def _():
        wait_c(2 * TILES - 1)

    @pl.when(jnp.logical_not(owner))
    def _():
        wait_c(2 * TILES)

    square = jnp.zeros((TOKENS, LANES), jnp.float32)
    for j in range(TILES):
        halves = [c_in[2 * j].astype(jnp.float32), c_in[2 * j + 1].astype(jnp.float32)]
        state = jnp.concatenate(halves * 4, axis=0)
        state = jnp.where(same_head, state, 0.0).astype(jnp.bfloat16)
        term = jnp.dot(qb[:, lanes(j)], state, preferred_element_type=jnp.float32)
        readout[:, lanes(j)] = term
        square = square + term * term
    mean_square = jnp.sum(square, axis=-1, keepdims=True) * (1.0 / D)
    scale = lax.rsqrt(mean_square + EPS)
    for j in range(TILES):
        normed = readout[:, lanes(j)] * scale * gain_ref[lanes(j)].reshape(1, LANES)
        mix[:, lanes(j)] = (normed + local[:, lanes(j)]).astype(jnp.bfloat16)
    for n in range(3):
        cols = pl.ds(n * 3 * LANES, 3 * LANES)
        result = jnp.dot(mix[...], wo_flat[:, cols], preferred_element_type=jnp.float32)
        result = result.astype(jnp.bfloat16)
        for k in range(3):
            out_ref[:, tile_lanes(slot_tile[3 * n + k])] = result[:, k * LANES : (k + 1) * LANES]

    def sent(ref, sem):
        remote(ref, ref, sem, sem, sibling).wait_send()

    sent(wkv.at[0:15], kv_s.at[0])
    sent(wqo.at[0:15], qo_s.at[0])

    @pl.when(owner)
    def _():
        sent(part_low.at[0:9], a_s.at[0])
        sent(c_all.at[0 : 2 * NZ - 1], c_s.at[0])
        for n in range(1, NZ):
            @pl.when(chip + n == NZ - 1)
            def _():
                sent(b_in.at[0:n], b_s.at[0])

    @pl.when(jnp.logical_not(owner))
    def _():
        sent(part_low, a_s.at[0])

    @pl.when(z < NZ - 1)
    def _():
        down.wait_send()

    @pl.when(z > 0)
    def _():
        up.wait_send()

    sent(wqo, o_s.at[0])


def per_device(video_tokens, qkv_weight, out_weight, conv_weight, norm_gain):
    tokens = video_tokens.reshape(TOKENS, D)
    bf16, f32 = jnp.bfloat16, jnp.float32
    vmem = pl.BlockSpec(memory_space=pltpu.VMEM)
    hbm = pl.BlockSpec(memory_space=pltpu.HBM)
    dma = pltpu.SemaphoreType.DMA
    operands = [
        pltpu.with_memory_space_constraint(a, pltpu.HBM)
        for a in (tokens, qkv_weight, out_weight, conv_weight, norm_gain)
    ]
    result = pl.pallas_call(
        kernel,
        out_shape=jax.ShapeDtypeStruct((TOKENS, D), bf16),
        in_specs=[hbm] * 4 + [vmem],
        out_specs=vmem,
        scratch_shapes=[
            pltpu.VMEM((NZ, ROWS, D), bf16),
            pltpu.VMEM((NZ, ROWS, D), bf16),
            pltpu.VMEM((NZ, ROWS, D), bf16),
            pltpu.VMEM((D, D), bf16),
            pltpu.VMEM((3, 3, D), f32),
            pltpu.VMEM((TOKENS, D), bf16),
            pltpu.VMEM((TOKENS, D), bf16),
            pltpu.VMEM((NZ, 2 * TOKENS, ROWS), bf16),
            pltpu.VMEM((2 * TOKENS, D), f32),
            pltpu.VMEM((2 * TOKENS, D), bf16),
            pltpu.VMEM((TOKENS, D), bf16),
            pltpu.VMEM((TOKENS, 5 * LANES), bf16),
            pltpu.VMEM((ROWS, LANES), bf16),
            pltpu.VMEM((TOKENS, LANES), bf16),
            pltpu.VMEM((2 * NZ, 16, LANES), bf16),
            pltpu.VMEM((TOKENS, D), bf16),
            pltpu.VMEM((2, COLS, D), bf16),
            pltpu.VMEM((TOKENS, D), f32),
            pltpu.VMEM((10, 2, 16, LANES), bf16),
            pltpu.VMEM((2 * NZ, 2, 16, LANES), bf16),
            pltpu.VMEM((2, 16, LANES), f32),
            pltpu.VMEM((NZ - 1, 16, LANES), bf16),
            pltpu.VMEM((16, LANES), bf16),
            pltpu.VMEM((2 * TILES, 16, LANES), bf16),
            pltpu.VMEM((2, 16, LANES), bf16),
            pltpu.VMEM((TOKENS, D), f32),
            pltpu.VMEM((TOKENS, D), bf16),
            dma((2, 8, 3)), dma((2, 8)), dma((2, 8)), dma((4,)),
            dma((1,)), dma((1,)), dma((5,)),
            dma((2,)), dma((4,)), dma((1,)), dma((4,)),
            dma((2,)), dma((2,)),
            dma((1,)), dma((1,)), dma((1,)), dma((1,)), dma((1,)), dma((1,)),
        ],
        compiler_params=pltpu.CompilerParams(
            collective_id=0, has_side_effects=True, vmem_limit_bytes=48 * 2**20
        ),
        name="block",
    )(*operands)
    return result.reshape(video_tokens.shape)


def solution(mesh):
    in_specs = (P("tm", "space", None, None), P("space", None), P("space", None), P(), P())
    out_specs = P("tm", "space", None, None)
    return jax.shard_map(
        per_device, mesh=mesh, in_specs=in_specs, out_specs=out_specs, check_vma=False
    )
```
